128 devices in a mesh: gx: 8 (over x, y_lo), gy: 16 (over y_hi, z, core).
Axes of the slice: x: 4, y: 4 (y_hi: 2, y_lo: 2; y = y_hi * 2 + y_lo), z: 4, core: 2. Of those that a mesh axis runs over, the one named last changes fastest.
Arguments:
- biomass: float32 [256, 256, 2048], P(None, 'gx', 'gy'), may hold values from 0.05 to 2
- capacity: float32 [256, 2048], P('gx', 'gy'), may hold values from 0.5 to 4
- adjacency: int32 [256, 256], replicated, may hold values 0 or 1
- trophic_level: int32 [256], replicated, may hold values from 0 to 3
- attack: float32 [256], replicated, may hold values from 0.05 to 0.5
- disp_rate: float32 [256], replicated, may hold values from 0.5 to 6
- disp_len: float32 [256], replicated, may hold values from 50 to 400
Outputs:
- advanced: float32 [256, 256, 2048], P(None, 'gx', 'gy')
The draws below stay inside these ranges and needn't reach their ends.
Inputs may be any that keep to these rules, and one draw needn't show every extreme that they name: `adjacency`: 0/1 feeding links.
All inputs are finite; a program needn't handle non-finite values.
Results may differ from the reference program's by a relative error of at most 0.000071.
Values sent between devices are 32-bit elements; how exact they have to be, the bound alone decides.
No kernel may reach another device: no remote copies, remote signals or barrier semaphores. Data moves between devices by JAX's collectives and lax.ppermute only.
A program may use at most 128 MiB of HBM per device.

```python
import math
import jax
import jax.numpy as jnp
from jax import lax

S = 256
NX = 256
NY = 2048


def with_ends(values, own_key, smallest, top_value):
    dims = values.shape
    spot = [jax.random.randint(jax.random.fold_in(own_key, axis), (), 0, dims[axis]) for axis in range(len(dims))]
    values = values.at[tuple(spot)].set(smallest)
    longest = dims.index(max(dims))
    spot[longest] = (spot[longest] + 1) % dims[longest]
    return values.at[tuple(spot)].set(top_value)


def shard_levels(stream_key, shape, cuts, least, largest):
    level, own = 1.0, jax.random.fold_in(stream_key, 6)
    for dim, shards_of in cuts:
        draws = jnp.exp(jax.random.uniform(jax.random.fold_in(own, dim), (shards_of,), jnp.float32, least / len(cuts), largest / len(cuts)))
        level = level * jnp.repeat(draws, shape[dim] // shards_of).reshape([-1 if axis == dim else 1 for axis in range(len(shape))])
    return level


def setup_inputs(seed: int = 0) -> dict:
    arg_keys = jax.random.split(jax.random.key(seed), 8)
    biomass = jnp.clip(0.05 + 1.95 * jax.random.uniform(arg_keys[0], (S, NX, NY), jnp.float32) ** shard_levels(arg_keys[0], (S, NX, NY), ((1, 8), (2, 16)), -0.2, 0.2), 0.05, 2.0)
    capacity = jnp.clip(jnp.exp(math.log(4.0) - 2.0794415 * jax.random.uniform(arg_keys[1], (NX, NY), jnp.float32) ** shard_levels(arg_keys[1], (NX, NY), ((0, 8), (1, 16)), -0.2, 0.2)), 0.5, 4.0)
    adjacency = with_ends((jax.random.randint(arg_keys[2], (S, S), 0, 8) < 1).astype(jnp.int32), jax.random.fold_in(arg_keys[2], 1), 0, 1)
    trophic_level = with_ends(jax.random.randint(arg_keys[3], (S,), 0, 4), jax.random.fold_in(arg_keys[3], 1), 0, 3).astype(jnp.int32)
    attack = jnp.clip(jnp.exp(jax.random.uniform(arg_keys[4], (S,), jnp.float32, math.log(0.05), math.log(0.5))), 0.05, 0.5)
    disp_rate = jnp.clip(jnp.exp(jax.random.uniform(arg_keys[5], (S,), jnp.float32, math.log(0.5), math.log(6.0))), 0.5, 6.0)
    disp_len = jnp.clip(jnp.exp(jax.random.uniform(arg_keys[6], (S,), jnp.float32, math.log(50.0), math.log(400.0))), 50.0, 400.0)
    return dict(biomass=biomass, capacity=capacity, adjacency=adjacency, trophic_level=trophic_level, attack=attack, disp_rate=disp_rate, disp_len=disp_len)


time_step = 0.25
handling = 1.0
efficiency = 0.6
mortal_rate = 0.15


def sweep(values, decay, scale, axis):
    moved = jnp.moveaxis(values, axis, 1)
    moved = jnp.moveaxis(moved, 1, 0)
    factor = decay[:, None]

    def advance(carry, column):
        carry = column + factor * carry
        return carry, carry

    start = jnp.zeros(moved.shape[1:], jnp.float32)
    forward = lax.scan(advance, start, moved)[1]
    backward = lax.scan(advance, start, moved, reverse=True)[1]
    total = forward + backward - moved
    total = jnp.moveaxis(total, 0, 1)
    total = jnp.moveaxis(total, 1, axis)
    return scale[:, None, None] * total


def respond(biomass, capacity, weights, basal, level_float):
    species = biomass.shape[0]
    flattened = biomass.reshape(species, -1)
    positive = jnp.maximum(flattened, 0.0)
    grazing = jnp.dot(weights.T, positive, precision=lax.Precision.HIGHEST, preferred_element_type=jnp.float32)
    handled = positive / (1.0 + handling * grazing)
    losses = positive * jnp.dot(weights, handled, precision=lax.Precision.HIGHEST, preferred_element_type=jnp.float32)
    growth = basal[:, None] * positive * (1.0 - positive / capacity.reshape(1, -1))
    result = growth + efficiency * handled * grazing - losses - mortal_rate * level_float[:, None] * positive
    return result.reshape(biomass.shape)


def reference(biomass, capacity, adjacency, trophic_level, attack, disp_rate, disp_len):
    decay = jnp.exp(-1.0 / disp_len)
    scale = (1.0 - decay) / (1.0 + decay)
    weights = adjacency.astype(jnp.float32) * attack[None, :]
    basal = (trophic_level == 0).astype(jnp.float32)
    level_float = trophic_level.astype(jnp.float32)

    def evaluate(state):
        smooth = sweep(sweep(state, decay, scale, 1), decay, scale, 2)
        return respond(state, capacity, weights, basal, level_float) + disp_rate[:, None, None] * (smooth - state)

    first = evaluate(biomass)
    middle = biomass + time_step * first
    second = evaluate(middle)
    return biomass + 0.5 * time_step * (first + second)
```

```python
import functools

import jax
import jax.numpy as jnp
from jax import lax
from jax.experimental import pallas as pl
from jax.experimental.pallas import tpu as pltpu
from jax.sharding import PartitionSpec as P

time_step = 0.25
handling = 1.0
efficiency = 0.6
mortal_rate = 0.15

S = 256
NXL = 32
NYL = 128
CH = 64
BX = 8
F32 = jnp.float32
BF16 = jnp.bfloat16
VMEM_LIMIT = 56 * 1024 * 1024


LAM, DEC, NORM2, RATE, ATT, BASAL, LEVEL = range(7)


def col(cols, k):
    return cols[:, k : k + 1]


def lanes(rows):
    return lax.broadcasted_iota(jnp.int32, (rows, NYL), 1)


def wide(column):
    return jnp.broadcast_to(column, (column.shape[0], NYL))


def powers(lam, exponent):
    return jnp.exp(-lam * exponent)


def tables(lam):
    y = lanes(lam.shape[0]).astype(F32) - 64.0
    return jnp.exp(-lam * y), jnp.exp(lam * y)


def second_tables(lam, dec):
    y = lanes(lam.shape[0]).astype(F32)
    inv = 1.0 / ((1.0 - dec) * (1.0 + dec))
    alpha = (y + 1.0) * jnp.exp(-lam * (y + 1.0)) + (jnp.exp(-lam * (y + 3.0)) - jnp.exp(-lam * (257.0 - y))) * inv
    beta = (128.0 - y) * jnp.exp(-lam * (128.0 - y)) + (jnp.exp(-lam * (130.0 - y)) - jnp.exp(-lam * (130.0 + y))) * inv
    return alpha, beta


def split(v):
    hi = v.astype(BF16)
    lo = (v - hi.astype(F32)).astype(BF16)
    return jnp.concatenate([hi, lo], axis=1)


def triangles():
    i = lax.broadcasted_iota(jnp.int32, (2 * NYL, NYL), 0) % NYL
    j = lax.broadcasted_iota(jnp.int32, (2 * NYL, NYL), 1)
    return (i <= j).astype(F32).astype(BF16), (i > j).astype(F32).astype(BF16)


def smooth_rows(v, a, ia, low, upp):
    f = jnp.dot(split(v * ia), low, preferred_element_type=F32)
    g = jnp.dot(split(v * a), upp, preferred_element_type=F32)
    return f * a + g * ia


def respond(v, rcap, adj, adj_t, att, basal, level):
    p = jnp.maximum(v, 0.0)
    both = jnp.dot(adj_t, split(p), preferred_element_type=F32)
    grazing = att * (both[:, :NYL] + both[:, NYL:])
    den = 1.0 + handling * grazing
    handled = p / den
    back = jnp.dot(adj, split(att * handled), preferred_element_type=F32)
    loss = back[:, :NYL] + back[:, NYL:]
    return p * (basal - mortal_rate * level - basal * p * rcap - loss) + efficiency * handled * grazing


def write_messages(msg_ref, front, back, lam, me, count, width):
    for k in range(count):
        gap = k - me
        dist = (jnp.abs(gap) - 1).astype(F32) * width
        w = jnp.exp(-lam * dist)
        picked = jnp.where(gap > 0, front, back)
        msg_ref[k] = jnp.where(gap == 0, 0.0, picked * w)


def read_carries(rx_ref, me, count):
    cf = jnp.zeros(rx_ref.shape[1:], F32)
    cb = jnp.zeros(rx_ref.shape[1:], F32)
    for k in range(count):
        m = rx_ref[k]
        cf = cf + jnp.where(k < me, m, 0.0)
        cb = cb + jnp.where(k > me, m, 0.0)
    return cf, cb


def fetch(b_hbm, bt, sems):
    for x in range(NXL):
        pltpu.make_async_copy(b_hbm.at[:, x, :], bt.at[x], sems.at[x]).start()


def fetched(b_hbm, bt, sems, x):
    pltpu.make_async_copy(b_hbm.at[:, x, :], bt.at[x], sems.at[x]).wait()


def tails_kernel(b_hbm, cols_ref, msg_ref, bt, fr, ba, sems):
    fetch(b_hbm, bt, sems)
    me = lax.axis_index("gx")
    for x0 in range(0, NXL, BX):
        for x in range(x0, x0 + BX):
            fetched(b_hbm, bt, sems, x)
        for s0 in range(0, S, CH):
            rows = pl.ds(s0, CH)
            lam = cols_ref[rows, LAM : LAM + 1]
            d = wide(cols_ref[rows, DEC : DEC + 1])
            vs = [bt[x, rows, :] for x in range(x0, x0 + BX)]
            f = fr[rows, :] if x0 else jnp.zeros((CH, NYL), F32)
            for v in vs:
                f = v + d * f
            g = vs[-1]
            for v in vs[-2::-1]:
                g = v + d * g
            fr[rows, :] = f
            if x0:
                ba[rows, :] = ba[rows, :] + powers(lam, float(x0)) * g
            else:
                ba[rows, :] = g
    write_messages(msg_ref, fr[...], ba[...], col(cols_ref[...], LAM), me, 8, float(NXL))


def first_kernel(b_hbm, adj_ref, cap_ref, cols_ref, q_ref, u_ref, fun_ref, bt, sems):
    fetch(b_hbm, bt, sems)
    cols = cols_ref[...]
    adj32 = adj_ref[...].astype(F32)
    adj = adj32.astype(BF16)
    adj_t = adj32.T.astype(BF16)
    att, basal, level, rate = (wide(col(cols, k)) for k in (ATT, BASAL, LEVEL, RATE))
    for x in range(NXL):
        fetched(b_hbm, bt, sems, x)

    def response(x, _):
        v = bt[x]
        rcap = 1.0 / cap_ref[pl.ds(x, 1), :]
        r = respond(v, rcap, adj, adj_t, att, basal, level)
        q_ref[x] = v + time_step * (r - rate * v)
        return 0

    lax.fori_loop(0, NXL, response, 0)

    def chunk(i, _):
        s0 = pl.multiple_of(i * CH, CH)
        rows = pl.ds(s0, CH)
        d = wide(cols_ref[rows, DEC : DEC + 1])
        lam = cols_ref[rows, LAM : LAM + 1]
        c = time_step * cols_ref[rows, RATE : RATE + 1] * cols_ref[rows, NORM2 : NORM2 + 1]
        y = lanes(CH).astype(F32)
        wf = jnp.exp(-lam * (127.0 - y))
        wb = jnp.exp(-lam * y)
        alpha, beta = second_tables(lam, cols_ref[rows, DEC : DEC + 1])
        inv_d = jnp.exp(lam)
        hf = c * beta * inv_d
        hb = c * alpha * inv_d
        lane = lanes(CH)

        def fwd(k, f):
            for j in range(BX):
                x = k * BX + j
                f = bt[x, rows, :] + d * f
                u_ref[x, rows, :] = f
            return f

        lax.fori_loop(0, NXL // BX, fwd, jnp.zeros((CH, NYL), F32))

        def bwd(k, carry):
            g, acc = carry
            for j in range(BX):
                x = NXL - 1 - (k * BX + j)
                g = d * g
                u = u_ref[x, rows, :] + g
                u_ref[x, rows, :] = u
                g = g + bt[x, rows, :]
                q = q_ref[x, rows, :]
                f1 = jnp.sum(wf * u, axis=1, keepdims=True)
                b1 = jnp.sum(wb * u, axis=1, keepdims=True)
                f2 = jnp.sum(wf * q + hf * u, axis=1, keepdims=True)
                b2 = jnp.sum(wb * q + hb * u, axis=1, keepdims=True)
                acc = jnp.where(lane == x, f1, acc)
                acc = jnp.where(lane == x + 32, f2, acc)
                acc = jnp.where(lane == x + 64, b1, acc)
                acc = jnp.where(lane == x + 96, b2, acc)
            return g, acc

        zero = jnp.zeros((CH, NYL), F32)
        _, acc = lax.fori_loop(0, NXL // BX, bwd, (zero, zero))
        fun_ref[rows, :] = acc
        return 0

    lax.fori_loop(0, S // CH, chunk, 0)


def by_group(lane, parts):
    out = parts[3]
    for k in (2, 1, 0):
        out = jnp.where(lane < 32 * (k + 1), parts[k], out)
    return out


def rows_kernel(rx_ref, fun_ref, cols_ref, car_ref, own_ref, msg_ref):
    mx, my = lax.axis_index("gx"), lax.axis_index("gy")
    cols = cols_ref[...]
    lam, dec = col(cols, LAM), col(cols, DEC)
    c = time_step * col(cols, RATE) * col(cols, NORM2)
    cf, cb = read_carries(rx_ref, mx, 8)
    car_ref[0] = cf
    car_ref[1] = cb
    lane = lanes(S)
    y = lane.astype(F32)
    wf = jnp.exp(-lam * (127.0 - y))
    wb = jnp.exp(-lam * y)
    alpha, beta = second_tables(lam, dec)
    inv_d = jnp.exp(lam)
    ws = (wf, c * beta * inv_d, wb, c * alpha * inv_d)
    pf = by_group(lane, [jnp.sum(w * cf, axis=1, keepdims=True) for w in ws])
    pb = by_group(lane, [jnp.sum(w * cb, axis=1, keepdims=True) for w in ws])
    xl = (lane % 32).astype(F32)
    fun = fun_ref[...] + jnp.exp(-lam * (xl + 1.0)) * pf + jnp.exp(-lam * (32.0 - xl)) * pb
    own_ref[...] = fun
    below, above = my.astype(F32), (15 - my).astype(F32)
    scale = c * dec / ((1.0 - dec) * (1.0 + dec)) * jnp.exp(-128.0 * lam)
    tb = scale * (1.0 - jnp.exp(-256.0 * below * lam))
    ta = scale * (1.0 - jnp.exp(-256.0 * above * lam))
    turned = pltpu.roll(fun, 96, 1)
    zero = jnp.zeros((S, 1), F32)
    fun = fun + by_group(lane, [zero, tb, zero, ta]) * turned
    shifted = by_group(lane, [zero, c * 128.0, zero, c * 128.0]) * pltpu.roll(fun, 32, 1)
    half = S // 2
    low_lanes = lanes(half) < 64

    def pack_front(v):
        return jnp.where(low_lanes, v[:half], pltpu.roll(v[half:], 64, 1))

    def pack_back(v):
        return jnp.where(low_lanes, pltpu.roll(v[:half], 64, 1), v[half:])

    f0, f1, b0, b1 = pack_front(fun), pack_front(shifted), pack_back(fun), pack_back(shifted)
    lam_p = jnp.where(low_lanes, lam[:half], lam[half:])
    for k in range(16):
        gap = k - my
        dist = (jnp.abs(gap) - 1).astype(F32)
        w = jnp.exp(-lam_p * (dist * 128.0))
        base = jnp.where(gap > 0, f0, b0) + dist * jnp.where(gap > 0, f1, b1)
        msg_ref[k] = jnp.where(gap == 0, 0.0, w * base)


def local_kernel(u_ref, q_ref, car_ref, cols_ref, mid_ref, p_ref, tail_ref, pf_ref, pb_ref):
    cols = cols_ref[...]
    lam = col(cols, LAM)
    c = wide(time_step * col(cols, RATE) * col(cols, NORM2))
    d = wide(col(cols, DEC))
    a, ia = tables(lam)
    low, upp = triangles()
    tail_ref[...] = jnp.zeros_like(tail_ref)
    pf_ref[...] = d
    pb_ref[...] = wide(jnp.exp(-32.0 * lam))
    inv_d = wide(jnp.exp(lam))

    def step(x, _):
        up, down = pf_ref[...], pb_ref[...]
        u = u_ref[x] + up * car_ref[0] + down * car_ref[1]
        mid = q_ref[x] + c * smooth_rows(u, a, ia, low, upp)
        mid_ref[x] = mid
        p = smooth_rows(mid, a, ia, low, upp)
        p_ref[x] = p
        tail_ref[0] = p + d * tail_ref[0]
        tail_ref[1] = tail_ref[1] + up * inv_d * p
        pf_ref[...] = up * d
        pb_ref[...] = down * inv_d
        return 0

    lax.fori_loop(0, NXL, step, 0)


def columns_kernel(ry_ref, own_ref, tail_ref, cols_ref, coef_ref, msg_ref):
    mx, my = lax.axis_index("gx"), lax.axis_index("gy")
    cols = cols_ref[...]
    lam, dec = col(cols, LAM), col(cols, DEC)
    c = time_step * col(cols, RATE) * col(cols, NORM2)
    lo, hi = read_carries(ry_ref, my, 16)
    half = S // 2
    low_lanes = lanes(half) < 64
    top = jnp.where(low_lanes, lo, pltpu.roll(hi, 64, 1))
    bottom = jnp.where(low_lanes, pltpu.roll(lo, 64, 1), hi)
    coef = jnp.concatenate([top, bottom], axis=0)
    lane = lanes(S)
    below, above = my.astype(F32), (15 - my).astype(F32)
    scale = c * dec / ((1.0 - dec) * (1.0 + dec))
    tb = scale * (1.0 - jnp.exp(-256.0 * below * lam))
    ta = scale * (1.0 - jnp.exp(-256.0 * above * lam))
    zero = jnp.zeros((S, 1), F32)
    turned = pltpu.roll(own_ref[...] + jnp.exp(-128.0 * lam) * coef, 96, 1)
    coef = coef + by_group(lane, [zero, tb, zero, ta]) * turned
    coef_ref[...] = coef
    xl = (lane % 32).astype(F32)
    cfx = coef * jnp.exp(-lam * (31.0 - xl))
    cbx = coef * jnp.exp(-lam * xl)
    y = lane.astype(F32)
    alpha, beta = second_tables(lam, dec)
    tabs = (c * alpha, jnp.exp(-lam * (y + 1.0)), c * beta, jnp.exp(-lam * (128.0 - y)))
    front, back = tail_ref[0], tail_ref[1]
    for k in range(4):
        inside = (lane >= 32 * k) & (lane < 32 * (k + 1))
        front = front + jnp.sum(jnp.where(inside, cfx, 0.0), axis=1, keepdims=True) * tabs[k]
        back = back + jnp.sum(jnp.where(inside, cbx, 0.0), axis=1, keepdims=True) * tabs[k]
    write_messages(msg_ref, front, back, lam, mx, 8, float(NXL))


def second_kernel(b_hbm, adj_ref, cap_ref, cols_ref, mid_ref, p_ref, coef_ref, out_ref, bt, v_ref, roll_ref, sems):
    fetch(b_hbm, bt, sems)
    cols = cols_ref[...]
    lam = col(cols, LAM)
    adj32 = adj_ref[...].astype(F32)
    adj = adj32.astype(BF16)
    adj_t = adj32.T.astype(BF16)
    att, basal, level, rate = (wide(col(cols, k)) for k in (ATT, BASAL, LEVEL, RATE))
    c = wide(time_step * col(cols, RATE) * col(cols, NORM2))
    y = lanes(S).astype(F32)
    ef = jnp.exp(-lam * (y + 1.0))
    eb = jnp.exp(-lam * (128.0 - y))
    alpha, beta = second_tables(lam, col(cols, DEC))
    roll_ref[...] = coef_ref[...]
    for x in range(NXL):
        fetched(b_hbm, bt, sems, x)

    def response(x, _):
        coef = roll_ref[...]
        cfu, cfm, cbu, cbm = (coef[:, 32 * k : 32 * k + 1] for k in range(4))
        roll_ref[...] = pltpu.roll(coef, 127, 1)
        mid = mid_ref[x] + c * (cfu * ef + cbu * eb)
        v_ref[x] = p_ref[x] + c * (cfu * alpha + cbu * beta) + cfm * ef + cbm * eb
        rcap = 1.0 / cap_ref[pl.ds(x, 1), :]
        r = respond(mid, rcap, adj, adj_t, att, basal, level)
        out_ref[x] = 0.5 * (bt[x] + mid) + 0.5 * time_step * (r - rate * mid)
        return 0

    lax.fori_loop(0, NXL, response, 0)

    def chunk(i, _):
        s0 = pl.multiple_of(i * CH, CH)
        rows = pl.ds(s0, CH)
        d = wide(cols_ref[rows, DEC : DEC + 1])
        e = wide(0.5 * time_step * cols_ref[rows, RATE : RATE + 1] * cols_ref[rows, NORM2 : NORM2 + 1])

        def fwd(k, f):
            for j in range(BX):
                x = k * BX + j
                f = v_ref[x, rows, :] + d * f
                out_ref[x, rows, :] = out_ref[x, rows, :] + e * f
            return f

        lax.fori_loop(0, NXL // BX, fwd, jnp.zeros((CH, NYL), F32))

        def bwd(k, g):
            for j in range(BX):
                x = NXL - 1 - (k * BX + j)
                g = d * g
                out_ref[x, rows, :] = out_ref[x, rows, :] + e * g
                g = g + v_ref[x, rows, :]
            return g

        lax.fori_loop(0, NXL // BX, bwd, jnp.zeros((CH, NYL), F32))
        return 0

    lax.fori_loop(0, S // CH, chunk, 0)


def final_kernel(o_ref, rx_ref, cols_ref, out_hbm, cf_ref, cb_ref, buf, sems):
    cols = cols_ref[...]
    lam = col(cols, LAM)
    e = 0.5 * time_step * col(cols, RATE) * col(cols, NORM2)
    cf, cb = read_carries(rx_ref, lax.axis_index("gx"), 8)
    cf_ref[...] = cf * (e * col(cols, DEC))
    cb_ref[...] = cb * (e * jnp.exp(-32.0 * lam))
    copies = []
    for x0 in range(0, NXL, BX):
        for s0 in range(0, S, CH):
            rows = pl.ds(s0, CH)
            d = wide(cols_ref[rows, DEC : DEC + 1])
            inv_d = wide(jnp.exp(cols_ref[rows, LAM : LAM + 1]))
            f, g = cf_ref[rows, :], cb_ref[rows, :]
            for x in range(x0, x0 + BX):
                buf[x, rows, :] = o_ref[x, rows, :] + f + g
                f = f * d
                g = g * inv_d
            cf_ref[rows, :] = f
            cb_ref[rows, :] = g
        for x in range(x0, x0 + BX):
            copy = pltpu.make_async_copy(buf.at[x], out_hbm.at[:, x, :], sems.at[x])
            copy.start()
            copies.append(copy)
    for copy in copies:
        copy.wait()


VM = pl.BlockSpec(memory_space=pltpu.VMEM)
ANY = pl.BlockSpec(memory_space=pl.ANY)
FIELD = (NXL, S, NYL)


def call(kernel, in_specs, outs, out_specs, scratch, microseconds):
    cost = pl.CostEstimate(flops=int(microseconds * 1e9), bytes_accessed=int(microseconds * 2e6), transcendentals=0)
    return pl.pallas_call(
        kernel,
        out_shape=[jax.ShapeDtypeStruct(shape, F32) for shape in outs],
        in_specs=in_specs,
        out_specs=out_specs,
        scratch_shapes=scratch,
        cost_estimate=cost,
        compiler_params=pltpu.CompilerParams(vmem_limit_bytes=VMEM_LIMIT),
    )


def shards(biomass, capacity, adjacency, trophic_level, attack, disp_rate, disp_len):
    inverse = 1.0 / disp_len
    decay = jnp.exp(-inverse)
    norm = (1.0 - decay) / (1.0 + decay)
    basal = (trophic_level == 0).astype(F32)
    level = trophic_level.astype(F32)
    cols = jnp.stack([inverse, decay, norm * norm, disp_rate, attack, basal, level, level], axis=1)

    field = pltpu.VMEM(FIELD, F32)
    plane = pltpu.VMEM((S, NYL), F32)
    dma = pltpu.SemaphoreType.DMA((NXL,))

    (msg,) = call(tails_kernel, [ANY, VM], [(8, S, NYL)], [VM], [field, plane, plane, dma], 3)(biomass, cols)
    rx = lax.all_to_all(msg, "gx", 0, 0)
    q, u, fun = call(
        first_kernel, [ANY, VM, VM, VM], [FIELD, FIELD, (S, NYL)], [VM, VM, VM], [field, dma], 12
    )(biomass, adjacency, capacity, cols)
    car, own, msg = call(
        rows_kernel, [VM, VM, VM], [(2, S, NYL), (S, NYL), (16, S // 2, NYL)], [VM, VM, VM], [], 1
    )(rx, fun, cols)
    ry = lax.all_to_all(msg, "gy", 0, 0)
    mid, p, tail = call(
        local_kernel, [VM, VM, VM, VM], [FIELD, FIELD, (2, S, NYL)], [VM, VM, VM], [plane, plane], 12
    )(u, q, car, cols)
    coef, msg = call(
        columns_kernel, [VM, VM, VM, VM], [(S, NYL), (8, S, NYL)], [VM, VM], [], 1
    )(ry, own, tail, cols)
    rx = lax.all_to_all(msg, "gx", 0, 0)
    (part,) = call(
        second_kernel, [ANY, VM, VM, VM, VM, VM, VM], [FIELD], [VM], [field, field, plane, dma], 12
    )(biomass, adjacency, capacity, cols, mid, p, coef)
    (out,) = call(
        final_kernel, [VM, VM, VM], [(S, NXL, NYL)], [ANY], [plane, plane, field, dma], 3
    )(part, rx, cols)
    return out


def solution(mesh):
    return jax.shard_map(
        shards,
        mesh=mesh,
        in_specs=(P(None, "gx", "gy"), P("gx", "gy"), P(), P(), P(), P(), P()),
        out_specs=P(None, "gx", "gy"),
        check_vma=False,
    )
```

```python
import jax
import jax.numpy as jnp
from jax import lax
from jax.experimental import pallas as pl
from jax.experimental.pallas import tpu as pltpu
from jax.sharding import PartitionSpec as P

time_step = 0.25
handling = 1.0
efficiency = 0.6
mortal_rate = 0.15

S = 256
NXL = 32
NYL = 128
CH = 64
BX = 8
BR = 4
BL = 4
F32 = jnp.float32
BF16 = jnp.bfloat16
VMEM_LIMIT = 32 * 1024 * 1024


LAM, DEC, NORM2, RATE, ATT, BASAL, LEVEL = range(7)
HOP_X, HOP_Y, WF, FH, WB, BH, UP, DOWN, TURN, RUN = range(10)
GROUPS = (BH, WB, FH, WF)


def col(cols, k):
    return cols[:, k : k + 1]


def lanes(rows):
    return lax.broadcasted_iota(jnp.int32, (rows, NYL), 1)


def wide(column):
    return jnp.broadcast_to(column, (column.shape[0], NYL))


def lane_sum(v):
    return jnp.sum(v, axis=1, keepdims=True)


def split(v):
    hi = v.astype(BF16)
    lo = (v - hi.astype(F32)).astype(BF16)
    return jnp.concatenate([hi, lo], axis=1)


def triangles():
    i = lax.broadcasted_iota(jnp.int32, (2 * NYL, NYL), 0) % NYL
    j = lax.broadcasted_iota(jnp.int32, (2 * NYL, NYL), 1)
    return (i <= j).astype(F32).astype(BF16), (i > j).astype(F32).astype(BF16)


def smooth_rows(v, a, ia, low, upp):
    f = jnp.dot(split(v * ia), low, preferred_element_type=F32)
    g = jnp.dot(split(v * a), upp, preferred_element_type=F32)
    return f * a + g * ia


def respond(v, rcap, adj, adj_t, att, basal, level):
    p = jnp.maximum(v, 0.0)
    both = jnp.dot(adj_t, split(p), preferred_element_type=F32)
    grazing = att * (both[:, :NYL] + both[:, NYL:])
    handled = p / (1.0 + handling * grazing)
    back = jnp.dot(adj, split(att * handled), preferred_element_type=F32)
    loss = back[:, :NYL] + back[:, NYL:]
    return p * (basal - mortal_rate * level - basal * p * rcap - loss) + efficiency * handled * grazing


def food_web(adj_ref, cols):
    adj = adj_ref[...].astype(F32)
    return (adj.astype(BF16), adj.T.astype(BF16)) + tuple(wide(col(cols, k)) for k in (ATT, BASAL, LEVEL))


def read_carries(rx_ref, hop, me, count):
    cf = jnp.zeros(rx_ref.shape[1:], F32)
    cb = jnp.zeros(rx_ref.shape[1:], F32)
    for k in range(count):
        cf = jnp.where(k < me, rx_ref[k] + hop * cf, cf)
    for k in range(count - 1, -1, -1):
        cb = jnp.where(k > me, rx_ref[k] + hop * cb, cb)
    return cf, cb


def write_messages(msg_ref, front, back, me, count):
    for k in range(count):
        msg_ref[k] = jnp.where(k > me, front, back)


def column_in(b_hbm, buf, sems, x):
    return pltpu.make_async_copy(b_hbm.at[:, x, :], buf.at[x], sems.at[x])


def plane_in(hbm, buf, sems, x):
    return pltpu.make_async_copy(hbm.at[x], buf.at[x], sems.at[x])


def plane_out(buf, hbm, sems, x):
    return pltpu.make_async_copy(buf.at[x], hbm.at[x], sems.at[x])


def chunk_out(buf, hbm, sems, i):
    part = pl.ds(pl.multiple_of(i * CH, CH), CH)
    return pltpu.make_async_copy(buf.at[:, part, :], hbm.at[:, part, :], sems.at[i])


def each(first, last, act):
    def body(k, _):
        act(k)
        return 0

    lax.fori_loop(first, last, body, 0)


def tails_kernel(b_hbm, level_hbm, attack_hbm, rate_hbm, length_hbm, cols_ref, msg_ref, bt, level, vec, fr, ba, sems, vsems):
    sources = (length_hbm, rate_hbm, attack_hbm)
    small = [pltpu.make_async_copy(h, vec.at[pl.ds(k, 1), :], vsems.at[k]) for k, h in enumerate(sources)]
    small.append(pltpu.make_async_copy(level_hbm, level, vsems.at[3]))
    for copy in small:
        copy.start()
    copies = [column_in(b_hbm, bt, sems, x) for x in range(NXL)]
    for copy in copies:
        copy.start()
    for copy in small:
        copy.wait()
    me = lax.axis_index("gx")
    lam = 1.0 / vec[0:1, :]
    dec = jnp.exp(-lam)
    norm = (1.0 - dec) / (1.0 + dec)
    basal = (level[...] == 0).astype(F32)
    rows = [lam, dec, norm * norm, vec[1:2, :], vec[2:3, :], basal, level[...].astype(F32)]
    cols_ref[...] = jnp.concatenate(rows + [jnp.zeros((NYL - len(rows), S), F32)], axis=0).T
    for x0 in range(0, NXL, BX):
        for x in range(x0, x0 + BX):
            copies[x].wait()
        for s0 in range(0, S, CH):
            part = pl.ds(s0, CH)
            d = wide(cols_ref[part, DEC : DEC + 1])
            vs = [bt[x, part, :] for x in range(x0, x0 + BX)]
            f = fr[part, :] if x0 else jnp.zeros((CH, NYL), F32)
            for v in vs:
                f = v + d * f
            g = vs[-1]
            for v in vs[-2::-1]:
                g = v + d * g
            if x0:
                g = ba[part, :] + wide(jnp.exp(-float(x0) * cols_ref[part, LAM : LAM + 1])) * g
            fr[part, :] = f
            ba[part, :] = g
    write_messages(msg_ref, fr[...], ba[...], me, 8)


def by_group(lane, parts):
    out = parts[3]
    for k in (2, 1, 0):
        out = jnp.where(lane < 32 * (k + 1), parts[k], out)
    return out


def fill_tables(tab_ref, cols, my):
    lam, dec = col(cols, LAM), col(cols, DEC)
    c = time_step * col(cols, RATE) * col(cols, NORM2)
    lane = lanes(S)
    y = lane.astype(F32)
    xl = (lane % 32).astype(F32)
    inv = 1.0 / ((1.0 - dec) * (1.0 + dec))
    wf = jnp.exp(-lam * (127.0 - y))
    wb = jnp.exp(-lam * y)
    tab_ref[HOP_X] = wide(jnp.exp(-32.0 * lam))
    tab_ref[HOP_Y] = wide(jnp.exp(-128.0 * lam))
    tab_ref[WF] = wf
    tab_ref[WB] = wb
    tab_ref[FH] = c * ((128.0 - y) * wf + (jnp.exp(-lam * (129.0 - y)) - jnp.exp(-lam * (129.0 + y))) * inv)
    tab_ref[BH] = c * ((y + 1.0) * wb + (jnp.exp(-lam * (y + 2.0)) - jnp.exp(-lam * (256.0 - y))) * inv)
    tab_ref[UP] = jnp.exp(-lam * (xl + 1.0))
    tab_ref[DOWN] = jnp.exp(-lam * (32.0 - xl))
    below, above = my.astype(F32), (15 - my).astype(F32)
    scale = c * dec * inv
    zero = jnp.zeros((S, 1), F32)
    tb = scale * (1.0 - jnp.exp(-256.0 * below * lam))
    ta = scale * (1.0 - jnp.exp(-256.0 * above * lam))
    tab_ref[TURN] = by_group(lane, [zero, tb, zero, ta])
    run = 128.0 * c
    tab_ref[RUN] = by_group(lane, [zero, run, zero, run])


def first_kernel(
    b_hbm, adj_ref, cap_ref, cols_ref, q_hbm, u_hbm, fun_ref, tab_ref, bt_ref, q_ref, u_ref, b_sems, q_sems, u_sems
):
    each(0, NXL, lambda x: column_in(b_hbm, bt_ref, b_sems, x).start())
    cols = cols_ref[...]
    fill_tables(tab_ref, cols, lax.axis_index("gy"))
    web = food_web(adj_ref, cols)
    rate = wide(col(cols, RATE))

    def response(i, _):
        for j in range(BR):
            x = i * BR + j
            column_in(b_hbm, bt_ref, b_sems, x).wait()
        for j in range(BR):
            x = i * BR + j
            v = bt_ref[x]
            rcap = 1.0 / cap_ref[pl.ds(x, 1), :]
            q_ref[x] = v + time_step * (respond(v, rcap, *web) - rate * v)
        for j in range(BR):
            plane_out(q_ref, q_hbm, q_sems, i * BR + j).start()
        return 0

    lax.fori_loop(0, NXL // BR, response, 0)

    def chunk(i, _):
        part = pl.ds(pl.multiple_of(i * CH, CH), CH)
        d = wide(cols_ref[part, DEC : DEC + 1])
        wf, hf, wb, hb = (tab_ref[k, part, :] for k in (WF, FH, WB, BH))
        lane = lanes(CH)

        def fwd(k, f):
            for j in range(BX):
                x = k * BX + j
                f = bt_ref[x, part, :] + d * f
                u_ref[x, part, :] = f
            return f

        lax.fori_loop(0, NXL // BX, fwd, jnp.zeros((CH, NYL), F32))

        def bwd(k, carry):
            g, acc = carry
            for j in range(BX):
                x = NXL - 1 - (k * BX + j)
                g = d * g
                u = u_ref[x, part, :] + g
                u_ref[x, part, :] = u
                g = g + bt_ref[x, part, :]
                q = q_ref[x, part, :]
                acc = jnp.where(lane == x, lane_sum(wf * u), acc)
                acc = jnp.where(lane == x + 32, lane_sum(wf * q + hf * u), acc)
                acc = jnp.where(lane == x + 64, lane_sum(wb * u), acc)
                acc = jnp.where(lane == x + 96, lane_sum(wb * q + hb * u), acc)
            return g, acc

        zero = jnp.zeros((CH, NYL), F32)
        fun_ref[part, :] = lax.fori_loop(0, NXL // BX, bwd, (zero, zero))[1]
        chunk_out(u_ref, u_hbm, u_sems, i).start()
        return 0

    lax.fori_loop(0, S // CH, chunk, 0)
    each(0, NXL, lambda x: plane_out(q_ref, q_hbm, q_sems, x).wait())
    each(0, S // CH, lambda i: chunk_out(u_ref, u_hbm, u_sems, i).wait())


def rows_kernel(rx_ref, fun_ref, tab_ref, car_ref, own_ref, msg_ref):
    mx, my = lax.axis_index("gx"), lax.axis_index("gy")
    cf, cb = read_carries(rx_ref, tab_ref[HOP_X], mx, 8)
    car_ref[0] = cf
    car_ref[1] = cb
    lane = lanes(S)
    pf = by_group(lane, [lane_sum(tab_ref[k] * cf) for k in (WF, FH, WB, BH)])
    pb = by_group(lane, [lane_sum(tab_ref[k] * cb) for k in (WF, FH, WB, BH)])
    fun = fun_ref[...] + tab_ref[UP] * pf + tab_ref[DOWN] * pb
    own_ref[...] = fun
    fun = fun + tab_ref[TURN] * tab_ref[HOP_Y] * pltpu.roll(fun, 96, 1)
    half = S // 2
    low_lanes = lanes(half) < 64
    front = jnp.where(low_lanes, fun[:half], pltpu.roll(fun[half:], 64, 1))
    back = jnp.where(low_lanes, pltpu.roll(fun[:half], 64, 1), fun[half:])
    write_messages(msg_ref, front, back, my, 16)


def local_kernel(
    u_hbm, q_hbm, car_ref, cols_ref, mid_hbm, p_hbm, tail_ref, u_ref, q_ref, up_ref, down_ref, u_sems, q_sems, p_sems, m_sems
):
    def fetch(x):
        plane_in(u_hbm, u_ref, u_sems, x).start()
        plane_in(q_hbm, q_ref, q_sems, x).start()

    each(0, NXL, fetch)
    cols = cols_ref[...]
    lam = col(cols, LAM)
    c = wide(time_step * col(cols, RATE) * col(cols, NORM2))
    d = wide(col(cols, DEC))
    inv_d = wide(jnp.exp(lam))
    y = lanes(S).astype(F32) - 64.0
    a, ia = jnp.exp(-lam * y), jnp.exp(lam * y)
    low, upp = triangles()
    tail_ref[...] = jnp.zeros_like(tail_ref)
    up_ref[...] = d
    down_ref[...] = wide(jnp.exp(-32.0 * lam))

    def step(i, _):
        for j in range(BL):
            plane_in(u_hbm, u_ref, u_sems, i * BL + j).wait()
            plane_in(q_hbm, q_ref, q_sems, i * BL + j).wait()
        for j in range(BL):
            x = i * BL + j
            up, down = up_ref[...], down_ref[...]
            u = u_ref[x] + up * car_ref[0] + down * car_ref[1]
            mid = q_ref[x] + c * smooth_rows(u, a, ia, low, upp)
            q_ref[x] = mid
            p = smooth_rows(mid, a, ia, low, upp)
            u_ref[x] = p
            tail_ref[0] = p + d * tail_ref[0]
            tail_ref[1] = tail_ref[1] + up * inv_d * p
            up_ref[...] = up * d
            down_ref[...] = down * inv_d
        for j in range(BL):
            plane_out(q_ref, mid_hbm, m_sems, i * BL + j).start()
            plane_out(u_ref, p_hbm, p_sems, i * BL + j).start()
        return 0

    lax.fori_loop(0, NXL // BL, step, 0)

    def drain(x):
        plane_out(q_ref, mid_hbm, m_sems, x).wait()
        plane_out(u_ref, p_hbm, p_sems, x).wait()

    each(0, NXL, drain)


def columns_kernel(ry_ref, own_ref, tail_ref, tab_ref, coef_ref, msg_ref):
    mx, my = lax.axis_index("gx"), lax.axis_index("gy")
    half = S // 2
    low_lanes = lanes(half) < 64
    hop = jnp.where(low_lanes, tab_ref[HOP_Y, :half, :], tab_ref[HOP_Y, half:, :])
    zero = jnp.zeros((half, NYL), F32)
    lo, lo2, hi, hi2 = zero, zero, zero, zero
    for k in range(15):
        lo2 = jnp.where(k < my, hop * (lo2 + lo), lo2)
        lo = jnp.where(k < my, ry_ref[k] + hop * lo, lo)
    for k in range(15, 0, -1):
        hi2 = jnp.where(k > my, hop * (hi2 + hi), hi2)
        hi = jnp.where(k > my, ry_ref[k] + hop * hi, hi)

    def unpack(low, high):
        top = jnp.where(low_lanes, low, pltpu.roll(high, 64, 1))
        bottom = jnp.where(low_lanes, pltpu.roll(low, 64, 1), high)
        return jnp.concatenate([top, bottom], axis=0)

    coef = unpack(lo, hi) + tab_ref[RUN] * pltpu.roll(unpack(lo2, hi2), 32, 1)
    coef = coef + tab_ref[TURN] * pltpu.roll(own_ref[...] + tab_ref[HOP_Y] * coef, 96, 1)
    coef_ref[...] = coef
    lane = lanes(S)
    at_front, at_back = coef * tab_ref[DOWN], coef * tab_ref[UP]
    front, back = tail_ref[0], tail_ref[1]
    for k, table in enumerate(GROUPS):
        inside = (lane >= 32 * k) & (lane < 32 * (k + 1))
        weight = tab_ref[table]
        front = front + lane_sum(jnp.where(inside, at_front, 0.0)) * weight
        back = back + lane_sum(jnp.where(inside, at_back, 0.0)) * weight
    write_messages(msg_ref, front, back, mx, 8)


def second_kernel(
    b_hbm, adj_ref, cap_ref, cols_ref, tab_ref, mid_hbm, p_hbm, coef_ref, out_hbm,
    out_ref, mid_ref, v_ref, roll_ref, b_sems, m_sems, p_sems, o_sems,
):
    def fetch(x):
        column_in(b_hbm, out_ref, b_sems, x).start()
        plane_in(mid_hbm, mid_ref, m_sems, x).start()
        plane_in(p_hbm, v_ref, p_sems, x).start()

    each(0, NXL, fetch)
    cols = cols_ref[...]
    web = food_web(adj_ref, cols)
    rate, d = wide(col(cols, RATE)), wide(col(cols, DEC))
    c = wide(time_step * col(cols, RATE) * col(cols, NORM2))
    ef, eb, alpha, beta = (d * tab_ref[k] for k in (WB, WF, BH, FH))
    roll_ref[...] = coef_ref[...]

    def response(i, _):
        for j in range(BR):
            x = i * BR + j
            column_in(b_hbm, out_ref, b_sems, x).wait()
            plane_in(mid_hbm, mid_ref, m_sems, x).wait()
            plane_in(p_hbm, v_ref, p_sems, x).wait()
        for j in range(BR):
            x = i * BR + j
            coef = roll_ref[...]
            cfu, cfm, cbu, cbm = (coef[:, 32 * k : 32 * k + 1] for k in range(4))
            roll_ref[...] = pltpu.roll(coef, 127, 1)
            mid = mid_ref[x] + c * (cfu * ef + cbu * eb)
            v_ref[x] = v_ref[x] + cfu * alpha + cbu * beta + cfm * ef + cbm * eb
            rcap = 1.0 / cap_ref[pl.ds(x, 1), :]
            r = respond(mid, rcap, *web)
            out_ref[x] = 0.5 * (out_ref[x] + mid) + 0.5 * time_step * (r - rate * mid)
        return 0

    lax.fori_loop(0, NXL // BR, response, 0)

    def chunk(i, _):
        part = pl.ds(pl.multiple_of(i * CH, CH), CH)
        d = wide(cols_ref[part, DEC : DEC + 1])
        e = wide(0.5 * time_step * cols_ref[part, RATE : RATE + 1] * cols_ref[part, NORM2 : NORM2 + 1])

        def fwd(k, f):
            for j in range(BX):
                x = k * BX + j
                f = v_ref[x, part, :] + d * f
                out_ref[x, part, :] = out_ref[x, part, :] + e * f
            return f

        lax.fori_loop(0, NXL // BX, fwd, jnp.zeros((CH, NYL), F32))

        def bwd(k, g):
            for j in range(BX):
                x = NXL - 1 - (k * BX + j)
                g = d * g
                out_ref[x, part, :] = out_ref[x, part, :] + e * g
                g = g + v_ref[x, part, :]
            return g

        lax.fori_loop(0, NXL // BX, bwd, jnp.zeros((CH, NYL), F32))
        chunk_out(out_ref, out_hbm, o_sems, i).start()
        return 0

    lax.fori_loop(0, S // CH, chunk, 0)
    each(0, S // CH, lambda i: chunk_out(out_ref, out_hbm, o_sems, i).wait())


def final_kernel(o_hbm, rx_ref, cols_ref, tab_ref, out_hbm, cf_ref, cb_ref, buf, in_sems, sems):
    loads = [plane_in(o_hbm, buf, in_sems, x) for x in range(NXL)]
    for copy in loads:
        copy.start()
    cols = cols_ref[...]
    lam = col(cols, LAM)
    e = 0.5 * time_step * col(cols, RATE) * col(cols, NORM2)
    cf, cb = read_carries(rx_ref, tab_ref[HOP_X], lax.axis_index("gx"), 8)
    cf_ref[...] = cf * (e * col(cols, DEC))
    cb_ref[...] = cb * (e * jnp.exp(-32.0 * lam))
    copies = [pltpu.make_async_copy(buf.at[x], out_hbm.at[:, x, :], sems.at[x]) for x in range(NXL)]
    for x0 in range(0, NXL, BX):
        for x in range(x0, x0 + BX):
            loads[x].wait()
        for s0 in range(0, S, CH):
            part = pl.ds(s0, CH)
            d = wide(cols_ref[part, DEC : DEC + 1])
            inv_d = wide(jnp.exp(cols_ref[part, LAM : LAM + 1]))
            f, g = cf_ref[part, :], cb_ref[part, :]
            for x in range(x0, x0 + BX):
                buf[x, part, :] = buf[x, part, :] + f + g
                f = f * d
                g = g * inv_d
            cf_ref[part, :] = f
            cb_ref[part, :] = g
        for x in range(x0, x0 + BX):
            copies[x].start()
    for copy in copies:
        copy.wait()


VM = pl.BlockSpec(memory_space=pltpu.VMEM)
HBM = pl.BlockSpec(memory_space=pltpu.HBM)
FIELD = (NXL, S, NYL)
PLANE = (S, NYL)


def in_vmem(x):
    return pltpu.with_memory_space_constraint(x, pltpu.VMEM)


def in_hbm(x):
    return pltpu.with_memory_space_constraint(x, pltpu.HBM)


def call(kernel, operands, outs, scratch, microseconds):
    cost = pl.CostEstimate(flops=int(microseconds * 1e9), bytes_accessed=int(microseconds * 2e6), transcendentals=0)
    return pl.pallas_call(
        kernel,
        out_shape=[shape for shape, _ in outs],
        in_specs=[spec for _, spec in operands],
        out_specs=[spec for _, spec in outs],
        scratch_shapes=scratch,
        cost_estimate=cost,
        compiler_params=pltpu.CompilerParams(vmem_limit_bytes=VMEM_LIMIT),
    )(*[in_hbm(x) if spec is HBM else x for x, spec in operands])


def shards(biomass, capacity, adjacency, trophic_level, attack, disp_rate, disp_len):
    field = pltpu.VMEM(FIELD, F32)
    plane = pltpu.VMEM(PLANE, F32)
    columns = pltpu.SemaphoreType.DMA((NXL,))
    chunks = pltpu.SemaphoreType.DMA((S // CH,))
    field_out = (pltpu.HBM(FIELD, F32), HBM)
    plane_out = (plane, VM)
    x_out = (pltpu.HBM((8,) + PLANE, F32), VM)
    y_out = (pltpu.HBM((16, S // 2, NYL), F32), VM)
    pair_out = (pltpu.VMEM((2,) + PLANE, F32), VM)
    tables_out = (pltpu.VMEM((10,) + PLANE, F32), VM)
    result = (pltpu.HBM((S, NXL, NYL), F32), HBM)

    vectors = [(v.reshape(1, S), HBM) for v in (trophic_level, attack, disp_rate, disp_len)]
    b = (biomass, HBM)
    adj, cap = (adjacency, VM), (capacity, VM)
    cols, msg = call(
        tails_kernel,
        [b] + vectors,
        [plane_out, x_out],
        [field, pltpu.VMEM((1, S), jnp.int32), pltpu.VMEM((8, S), F32), plane, plane, columns, pltpu.SemaphoreType.DMA((4,))],
        3,
    )
    cols = (in_vmem(cols), VM)
    rx = in_vmem(lax.all_to_all(msg, "gx", 0, 0))
    q, u, fun, tab = call(
        first_kernel,
        [b, adj, cap, cols],
        [field_out, field_out, plane_out, tables_out],
        [field, field, field, columns, columns, chunks],
        12,
    )
    tab = (in_vmem(tab), VM)
    car, own, msg = call(
        rows_kernel, [(rx, VM), (in_vmem(fun), VM), tab], [pair_out, plane_out, y_out], [], 1
    )
    ry = in_vmem(lax.all_to_all(msg, "gy", 0, 0))
    mid, p, tail = call(
        local_kernel,
        [(u, HBM), (q, HBM), (in_vmem(car), VM), cols],
        [field_out, field_out, pair_out],
        [field, field, plane, plane, columns, columns, columns, columns],
        12,
    )
    coef, msg = call(
        columns_kernel, [(ry, VM), (in_vmem(own), VM), (in_vmem(tail), VM), tab], [plane_out, x_out], [], 1
    )
    rx = in_vmem(lax.all_to_all(msg, "gx", 0, 0))
    (part,) = call(
        second_kernel,
        [b, adj, cap, cols, tab, (mid, HBM), (p, HBM), (in_vmem(coef), VM)],
        [field_out],
        [field, field, field, plane, columns, columns, columns, chunks],
        12,
    )
    (out,) = call(
        final_kernel, [(part, HBM), (rx, VM), cols, tab], [result], [plane, plane, field, columns, columns], 3
    )
    return out


def solution(mesh):
    return jax.shard_map(
        shards,
        mesh=mesh,
        in_specs=(P(None, "gx", "gy"), P("gx", "gy"), P(), P(), P(), P(), P()),
        out_specs=P(None, "gx", "gy"),
        check_vma=False,
    )
```

```python
import jax
import jax.numpy as jnp
from jax import lax
from jax.experimental import pallas as pl
from jax.experimental.pallas import tpu as pltpu
from jax.sharding import PartitionSpec as P

time_step = 0.25
handling = 1.0
efficiency = 0.6
mortal_rate = 0.15

S = 256
NXL = 32
NYL = 128
CH = 64
BX = 8
BR = 4
BL = 4
F32 = jnp.float32
BF16 = jnp.bfloat16
VMEM_LIMIT = 32 * 1024 * 1024


LAM, DEC, NORM2, RATE, ATT, BASAL, LEVEL = range(7)
HOP_X, HOP_Y, WF, FH, WB, BH, UP, DOWN, TURN, RUN = range(10)
GROUPS = (BH, WB, FH, WF)


def col(cols, k):
    return cols[:, k : k + 1]


def lanes(rows):
    return lax.broadcasted_iota(jnp.int32, (rows, NYL), 1)


def wide(column):
    return jnp.broadcast_to(column, (column.shape[0], NYL))


def lane_sum(v):
    return jnp.sum(v, axis=1, keepdims=True)


def split(v):
    hi = v.astype(BF16)
    lo = (v - hi.astype(F32)).astype(BF16)
    return jnp.concatenate([hi, lo], axis=1)


def triangles():
    i = lax.broadcasted_iota(jnp.int32, (2 * NYL, NYL), 0) % NYL
    j = lax.broadcasted_iota(jnp.int32, (2 * NYL, NYL), 1)
    return (i <= j).astype(F32).astype(BF16), (i > j).astype(F32).astype(BF16)


def smooth_rows(v, a, ia, low, upp):
    f = jnp.dot(split(v * ia), low, preferred_element_type=F32)
    g = jnp.dot(split(v * a), upp, preferred_element_type=F32)
    return f * a + g * ia


def smooth_and_total(v, a, ia, low, upp):
    f = jnp.dot(split(v * ia), low, preferred_element_type=F32)
    g = jnp.dot(split(v * a), upp, preferred_element_type=F32)
    return f[:, :NYL] * a + g[:, :NYL] * ia, f[:, NYL:], g[:, NYL:]


def respond(v, rcap, adj, adj_t, att, basal, level):
    p = jnp.maximum(v, 0.0)
    both = jnp.dot(adj_t, split(p), preferred_element_type=F32)
    grazing = att * (both[:, :NYL] + both[:, NYL:])
    handled = p / (1.0 + handling * grazing)
    back = jnp.dot(adj, split(att * handled), preferred_element_type=F32)
    loss = back[:, :NYL] + back[:, NYL:]
    return p * (basal - mortal_rate * level - basal * p * rcap - loss) + efficiency * handled * grazing


def food_web(adj_ref, cols):
    adj = adj_ref[...].astype(F32)
    return (adj.astype(BF16), adj.T.astype(BF16)) + tuple(wide(col(cols, k)) for k in (ATT, BASAL, LEVEL))


def read_carries(rx_ref, hop, me, count):
    cf = jnp.zeros(rx_ref.shape[1:], F32)
    cb = jnp.zeros(rx_ref.shape[1:], F32)
    for k in range(count):
        cf = jnp.where(k < me, rx_ref[k] + hop * cf, cf)
    for k in range(count - 1, -1, -1):
        cb = jnp.where(k > me, rx_ref[k] + hop * cb, cb)
    return cf, cb


def send_messages(sides, msg_hbm, sems, me, count):
    copies = [
        pltpu.make_async_copy(sides.at[(k > me).astype(jnp.int32)], msg_hbm.at[k], sems.at[k]) for k in range(count)
    ]
    for copy in copies:
        copy.start()
    for copy in copies:
        copy.wait()


def column_in(b_hbm, buf, sems, x):
    return pltpu.make_async_copy(b_hbm.at[:, x, :], buf.at[x], sems.at[x])


def plane_in(hbm, buf, sems, x):
    return pltpu.make_async_copy(hbm.at[x], buf.at[x], sems.at[x])


def plane_out(buf, hbm, sems, x):
    return pltpu.make_async_copy(buf.at[x], hbm.at[x], sems.at[x])


def chunk_out(buf, hbm, sems, i):
    part = pl.ds(pl.multiple_of(i * CH, CH), CH)
    return pltpu.make_async_copy(buf.at[:, part, :], hbm.at[:, part, :], sems.at[i])


def each(first, last, act):
    def body(k, _):
        act(k)
        return 0

    lax.fori_loop(first, last, body, 0)


def tails_kernel(b_hbm, level_hbm, attack_hbm, rate_hbm, length_hbm, cols_ref, msg_hbm, bt, level, vec, sides, sems, vsems, msems):
    sources = (length_hbm, rate_hbm, attack_hbm)
    small = [pltpu.make_async_copy(h, vec.at[pl.ds(k, 1), :], vsems.at[k]) for k, h in enumerate(sources)]
    small.append(pltpu.make_async_copy(level_hbm, level, vsems.at[3]))
    for copy in small:
        copy.start()
    copies = [column_in(b_hbm, bt, sems, x) for x in range(NXL)]
    for copy in copies:
        copy.start()
    for copy in small:
        copy.wait()
    me = lax.axis_index("gx")
    lam = 1.0 / vec[0:1, :]
    dec = jnp.exp(-lam)
    norm = (1.0 - dec) / (1.0 + dec)
    basal = (level[...] == 0).astype(F32)
    rows = [lam, dec, norm * norm, vec[1:2, :], vec[2:3, :], basal, level[...].astype(F32)]
    cols_ref[...] = jnp.concatenate(rows + [jnp.zeros((NYL - len(rows), S), F32)], axis=0).T
    for x0 in range(0, NXL, BX):
        for x in range(x0, x0 + BX):
            copies[x].wait()
        for s0 in range(0, S, CH):
            part = pl.ds(s0, CH)
            d = wide(cols_ref[part, DEC : DEC + 1])
            vs = [bt[x, part, :] for x in range(x0, x0 + BX)]
            f = sides[1, part, :] if x0 else jnp.zeros((CH, NYL), F32)
            for v in vs:
                f = v + d * f
            g = vs[-1]
            for v in vs[-2::-1]:
                g = v + d * g
            if x0:
                g = sides[0, part, :] + wide(jnp.exp(-float(x0) * cols_ref[part, LAM : LAM + 1])) * g
            sides[1, part, :] = f
            sides[0, part, :] = g
    send_messages(sides, msg_hbm, msems, me, 8)


def by_group(lane, parts):
    out = parts[3]
    for k in (2, 1, 0):
        out = jnp.where(lane < 32 * (k + 1), parts[k], out)
    return out


def fill_tables(tab_ref, cols, my):
    lam, dec = col(cols, LAM), col(cols, DEC)
    c = time_step * col(cols, RATE) * col(cols, NORM2)
    lane = lanes(S)
    y = lane.astype(F32)
    xl = (lane % 32).astype(F32)
    inv = 1.0 / ((1.0 - dec) * (1.0 + dec))
    wf = jnp.exp(-lam * (127.0 - y))
    wb = jnp.exp(-lam * y)
    tab_ref[HOP_X] = wide(jnp.exp(-32.0 * lam))
    tab_ref[HOP_Y] = wide(jnp.exp(-128.0 * lam))
    tab_ref[WF] = wf
    tab_ref[WB] = wb
    tab_ref[FH] = c * ((128.0 - y) * wf + (jnp.exp(-lam * (129.0 - y)) - jnp.exp(-lam * (129.0 + y))) * inv)
    tab_ref[BH] = c * ((y + 1.0) * wb + (jnp.exp(-lam * (y + 2.0)) - jnp.exp(-lam * (256.0 - y))) * inv)
    tab_ref[UP] = jnp.exp(-lam * (xl + 1.0))
    tab_ref[DOWN] = jnp.exp(-lam * (32.0 - xl))
    below, above = my.astype(F32), (15 - my).astype(F32)
    scale = c * dec * inv
    zero = jnp.zeros((S, 1), F32)
    tb = scale * (1.0 - jnp.exp(-256.0 * below * lam))
    ta = scale * (1.0 - jnp.exp(-256.0 * above * lam))
    tab_ref[TURN] = by_group(lane, [zero, tb, zero, ta])
    run = 128.0 * c
    tab_ref[RUN] = by_group(lane, [zero, run, zero, run])


def first_kernel(
    b_hbm, adj_ref, cap_ref, cols_ref, q_hbm, fun_ref, tab_ref, bt_ref, q_ref, u_ref, f_ref, b_sems, q_sems
):
    each(0, NXL, lambda x: column_in(b_hbm, bt_ref, b_sems, x).start())
    cols = cols_ref[...]
    fill_tables(tab_ref, cols, lax.axis_index("gy"))
    web = food_web(adj_ref, cols)
    rate, d = wide(col(cols, RATE)), wide(col(cols, DEC))
    f_ref[...] = jnp.zeros_like(f_ref)

    def response(i, _):
        for j in range(BR):
            x = i * BR + j
            column_in(b_hbm, bt_ref, b_sems, x).wait()
        for j in range(BR):
            x = i * BR + j
            v = bt_ref[x]
            rcap = 1.0 / cap_ref[pl.ds(x, 1), :]
            q_ref[x] = v + time_step * (respond(v, rcap, *web) - rate * v)
            f = v + d * f_ref[...]
            f_ref[...] = f
            u_ref[x] = f
        return 0

    lax.fori_loop(0, NXL // BR, response, 0)

    low, upp = triangles()
    ones = jnp.ones((2 * NYL, NYL), BF16)
    low, upp = jnp.concatenate([low, ones], axis=1), jnp.concatenate([upp, ones], axis=1)
    lam = col(cols, LAM)
    c = wide(time_step * col(cols, RATE) * col(cols, NORM2))
    lane = lanes(S)
    y = lane.astype(F32) - 64.0
    a, ia = jnp.exp(-lam * y), jnp.exp(lam * y)
    f_ref[...] = jnp.zeros_like(f_ref)
    fun_ref[...] = jnp.zeros_like(fun_ref)

    def smoothing(i, _):
        for j in range(BL):
            x = NXL - 1 - (i * BL + j)
            g = d * f_ref[...]
            u = u_ref[x] + g
            f_ref[...] = g + bt_ref[x]
            smooth, total_f, total_b = smooth_and_total(u, a, ia, low, upp)
            q = q_ref[x] + c * smooth
            q_ref[x] = q
            acc = jnp.where(lane == x, total_f, fun_ref[...])
            acc = jnp.where(lane == x + 32, lane_sum(tab_ref[WF] * q), acc)
            acc = jnp.where(lane == x + 64, total_b, acc)
            fun_ref[...] = jnp.where(lane == x + 96, lane_sum(tab_ref[WB] * q), acc)
        for j in range(BL):
            plane_out(q_ref, q_hbm, q_sems, NXL - 1 - (i * BL + j)).start()
        return 0

    lax.fori_loop(0, NXL // BL, smoothing, 0)
    one = jnp.ones_like(lam)
    fun_ref[...] = fun_ref[...] * by_group(lane, [jnp.exp(-63.0 * lam), one, jnp.exp(-64.0 * lam), one])
    each(0, NXL, lambda x: plane_out(q_ref, q_hbm, q_sems, x).wait())


def rows_kernel(rx_ref, fun_ref, tab_ref, car_ref, own_ref, sides, msg_hbm, msems):
    mx, my = lax.axis_index("gx"), lax.axis_index("gy")
    cf, cb = read_carries(rx_ref, tab_ref[HOP_X], mx, 8)
    car_ref[0] = cf
    car_ref[1] = cb
    lane = lanes(S)
    pf = by_group(lane, [lane_sum(tab_ref[k] * cf) for k in (WF, FH, WB, BH)])
    pb = by_group(lane, [lane_sum(tab_ref[k] * cb) for k in (WF, FH, WB, BH)])
    fun = fun_ref[...] + tab_ref[UP] * pf + tab_ref[DOWN] * pb
    own_ref[...] = fun
    fun = fun + tab_ref[TURN] * tab_ref[HOP_Y] * pltpu.roll(fun, 96, 1)
    half = S // 2
    low_lanes = lanes(half) < 64
    sides[1] = jnp.where(low_lanes, fun[:half], pltpu.roll(fun[half:], 64, 1))
    sides[0] = jnp.where(low_lanes, pltpu.roll(fun[:half], 64, 1), fun[half:])
    send_messages(sides, msg_hbm, msems, my // 2, 8)


def local_kernel(
    q_hbm, car_ref, cols_ref, mid_hbm, p_hbm, tail_ref, q_ref, p_ref, up_ref, down_ref, q_sems, p_sems, m_sems
):
    each(0, NXL, lambda x: plane_in(q_hbm, q_ref, q_sems, x).start())
    cols = cols_ref[...]
    lam = col(cols, LAM)
    c = wide(time_step * col(cols, RATE) * col(cols, NORM2))
    d = wide(col(cols, DEC))
    inv_d = wide(jnp.exp(lam))
    y = lanes(S).astype(F32) - 64.0
    a, ia = jnp.exp(-lam * y), jnp.exp(lam * y)
    low, upp = triangles()
    tail_ref[...] = jnp.zeros_like(tail_ref)
    up_ref[...] = c * d * smooth_rows(car_ref[0], a, ia, low, upp)
    down_ref[...] = c * jnp.exp(-32.0 * lam) * smooth_rows(car_ref[1], a, ia, low, upp)

    def step(i, weight):
        for j in range(BL):
            plane_in(q_hbm, q_ref, q_sems, i * BL + j).wait()
        for j in range(BL):
            x = i * BL + j
            up, down = up_ref[...], down_ref[...]
            mid = q_ref[x] + up + down
            q_ref[x] = mid
            p = smooth_rows(mid, a, ia, low, upp)
            p_ref[x] = p
            tail_ref[0] = p + d * tail_ref[0]
            tail_ref[1] = tail_ref[1] + weight * p
            up_ref[...] = up * d
            down_ref[...] = down * inv_d
            weight = weight * col(cols, DEC)
        for j in range(BL):
            plane_out(q_ref, mid_hbm, m_sems, i * BL + j).start()
            plane_out(p_ref, p_hbm, p_sems, i * BL + j).start()
        return weight

    lax.fori_loop(0, NXL // BL, step, jnp.ones((S, 1), F32))

    def drain(x):
        plane_out(q_ref, mid_hbm, m_sems, x).wait()
        plane_out(p_ref, p_hbm, p_sems, x).wait()

    each(0, NXL, drain)


def packed(low_lanes, v):
    return jnp.where(low_lanes, v[: S // 2], v[S // 2 :])


def chips_kernel(ry_ref, sides_ref, tab_ref, tail_ref, part_ref, msg_ref):
    my = lax.axis_index("gy")
    del tail_ref
    chip, core = my // 2, my % 2
    half = S // 2
    low_lanes = lanes(half) < 64
    hop = packed(low_lanes, tab_ref[HOP_Y])
    run = packed(low_lanes, tab_ref[RUN])
    hop2 = hop * hop
    zero = jnp.zeros((half, NYL), F32)
    lo, lo2, hi, hi2 = zero, zero, zero, zero
    for k in range(7):
        lo2 = jnp.where(k < chip, hop2 * (lo2 + lo), lo2)
        lo = jnp.where(k < chip, ry_ref[k] + hop2 * lo, lo)
    for k in range(7, 0, -1):
        hi2 = jnp.where(k > chip, hop2 * (hi2 + hi), hi2)
        hi = jnp.where(k > chip, ry_ref[k] + hop2 * hi, hi)

    def same(z, z2):
        return hop * z + run * pltpu.roll(hop * (2.0 * z2 + z), 32, 1)

    def near(z, z2):
        return z + run * pltpu.roll(2.0 * z2, 32, 1)

    def far(z, z2):
        return hop2 * z + run * pltpu.roll(2.0 * hop2 * (z2 + z), 32, 1)

    part_ref[0] = same(lo, lo2)
    part_ref[1] = same(hi, hi2)
    msg_ref[0] = jnp.where(core == 0, far(lo, lo2) + sides_ref[1], near(lo, lo2))
    msg_ref[1] = jnp.where(core == 1, far(hi, hi2) + sides_ref[0], near(hi, hi2))


def columns_kernel(part_ref, other_ref, own_ref, tail_ref, tab_ref, coef_ref, msg_hbm, sides, msems):
    mx = lax.axis_index("gx")
    low_lanes = lanes(S // 2) < 64
    lo = part_ref[0] + other_ref[0]
    hi = part_ref[1] + other_ref[1]
    top = jnp.where(low_lanes, lo, pltpu.roll(hi, 64, 1))
    bottom = jnp.where(low_lanes, pltpu.roll(lo, 64, 1), hi)
    coef = jnp.concatenate([top, bottom], axis=0)
    coef = coef + tab_ref[TURN] * pltpu.roll(own_ref[...] + tab_ref[HOP_Y] * coef, 96, 1)
    coef_ref[...] = coef
    lane = lanes(S)
    at_front, at_back = coef * tab_ref[DOWN], coef * tab_ref[UP]
    front, back = tail_ref[0], tail_ref[1]
    for k, table in enumerate(GROUPS):
        inside = (lane >= 32 * k) & (lane < 32 * (k + 1))
        weight = tab_ref[table]
        front = front + lane_sum(jnp.where(inside, at_front, 0.0)) * weight
        back = back + lane_sum(jnp.where(inside, at_back, 0.0)) * weight
    sides[1] = front
    sides[0] = back
    send_messages(sides, msg_hbm, msems, mx, 8)


def second_kernel(
    b_hbm, adj_ref, cap_ref, cols_ref, tab_ref, mid_hbm, p_hbm, coef_ref, out_hbm,
    out_ref, mid_ref, v_ref, roll_ref, f_ref, b_sems, m_sems, p_sems, o_sems,
):
    def fetch(x):
        column_in(b_hbm, out_ref, b_sems, x).start()
        plane_in(mid_hbm, mid_ref, m_sems, x).start()
        plane_in(p_hbm, v_ref, p_sems, x).start()

    each(0, NXL, fetch)
    cols = cols_ref[...]
    web = food_web(adj_ref, cols)
    rate, d = wide(col(cols, RATE)), wide(col(cols, DEC))
    c = wide(time_step * col(cols, RATE) * col(cols, NORM2))
    ef, eb, alpha, beta = (d * tab_ref[k] for k in (WB, WF, BH, FH))
    e = wide(0.5 * time_step * col(cols, RATE) * col(cols, NORM2))
    roll_ref[...] = coef_ref[...]
    f_ref[...] = jnp.zeros_like(f_ref)

    def response(i, _):
        for j in range(BR):
            x = i * BR + j
            column_in(b_hbm, out_ref, b_sems, x).wait()
            plane_in(mid_hbm, mid_ref, m_sems, x).wait()
            plane_in(p_hbm, v_ref, p_sems, x).wait()
        for j in range(BR):
            x = i * BR + j
            coef = roll_ref[...]
            cfu, cfm, cbu, cbm = (coef[:, 32 * k : 32 * k + 1] for k in range(4))
            roll_ref[...] = pltpu.roll(coef, 127, 1)
            mid = mid_ref[x] + c * (cfu * ef + cbu * eb)
            v = v_ref[x] + cfu * alpha + cbu * beta + cfm * ef + cbm * eb
            v_ref[x] = v
            f = v + d * f_ref[...]
            f_ref[...] = f
            rcap = 1.0 / cap_ref[pl.ds(x, 1), :]
            r = respond(mid, rcap, *web)
            out_ref[x] = 0.5 * (out_ref[x] + mid) + 0.5 * time_step * (r - rate * mid) + e * f
        return 0

    lax.fori_loop(0, NXL // BR, response, 0)

    def chunk(i, _):
        part = pl.ds(pl.multiple_of(i * CH, CH), CH)
        d = wide(cols_ref[part, DEC : DEC + 1])
        e = wide(0.5 * time_step * cols_ref[part, RATE : RATE + 1] * cols_ref[part, NORM2 : NORM2 + 1])

        def bwd(k, g):
            for j in range(BX):
                x = NXL - 1 - (k * BX + j)
                g = d * g
                out_ref[x, part, :] = out_ref[x, part, :] + e * g
                g = g + v_ref[x, part, :]
            return g

        lax.fori_loop(0, NXL // BX, bwd, jnp.zeros((CH, NYL), F32))
        chunk_out(out_ref, out_hbm, o_sems, i).start()
        return 0

    lax.fori_loop(0, S // CH, chunk, 0)
    each(0, S // CH, lambda i: chunk_out(out_ref, out_hbm, o_sems, i).wait())


def final_kernel(o_hbm, rx_ref, cols_ref, tab_ref, out_hbm, cf_ref, cb_ref, buf, in_sems, sems):
    loads = [plane_in(o_hbm, buf, in_sems, x) for x in range(NXL)]
    for copy in loads:
        copy.start()
    cols = cols_ref[...]
    lam = col(cols, LAM)
    e = 0.5 * time_step * col(cols, RATE) * col(cols, NORM2)
    cf, cb = read_carries(rx_ref, tab_ref[HOP_X], lax.axis_index("gx"), 8)
    cf_ref[...] = cf * (e * col(cols, DEC))
    cb_ref[...] = cb * (e * jnp.exp(-32.0 * lam))
    copies = [pltpu.make_async_copy(buf.at[x], out_hbm.at[:, x, :], sems.at[x]) for x in range(NXL)]
    for x0 in range(0, NXL, BX):
        for x in range(x0, x0 + BX):
            loads[x].wait()
        for s0 in range(0, S, CH):
            part = pl.ds(s0, CH)
            d = wide(cols_ref[part, DEC : DEC + 1])
            inv_d = wide(jnp.exp(cols_ref[part, LAM : LAM + 1]))
            f, g = cf_ref[part, :], cb_ref[part, :]
            for x in range(x0, x0 + BX):
                buf[x, part, :] = buf[x, part, :] + f + g
                f = f * d
                g = g * inv_d
            cf_ref[part, :] = f
            cb_ref[part, :] = g
        for x in range(x0, x0 + BX):
            copies[x].start()
    for copy in copies:
        copy.wait()


VM = pl.BlockSpec(memory_space=pltpu.VMEM)
HBM = pl.BlockSpec(memory_space=pltpu.HBM)
FIELD = (NXL, S, NYL)
PLANE = (S, NYL)


def in_vmem(x):
    return pltpu.with_memory_space_constraint(x, pltpu.VMEM)


def in_hbm(x):
    return pltpu.with_memory_space_constraint(x, pltpu.HBM)


def call(kernel, operands, outs, scratch, microseconds):
    cost = pl.CostEstimate(flops=int(microseconds * 1e9), bytes_accessed=int(microseconds * 2e6), transcendentals=0)
    return pl.pallas_call(
        kernel,
        out_shape=[shape for shape, _ in outs],
        in_specs=[spec for _, spec in operands],
        out_specs=[spec for _, spec in outs],
        scratch_shapes=scratch,
        cost_estimate=cost,
        compiler_params=pltpu.CompilerParams(vmem_limit_bytes=VMEM_LIMIT),
    )(*[in_hbm(x) if spec is HBM else x for x, spec in operands])


def shards(biomass, capacity, adjacency, trophic_level, attack, disp_rate, disp_len):
    field = pltpu.VMEM(FIELD, F32)
    plane = pltpu.VMEM(PLANE, F32)
    columns = pltpu.SemaphoreType.DMA((NXL,))
    chunks = pltpu.SemaphoreType.DMA((S // CH,))
    x_sides = [pltpu.VMEM((2,) + PLANE, F32), pltpu.SemaphoreType.DMA((8,))]
    same_core = [[core + 2 * chip for chip in range(8)] for core in range(2)]
    other_core = [(k, k ^ 1) for k in range(16)]
    field_out = (pltpu.HBM(FIELD, F32), HBM)
    plane_out = (plane, VM)
    x_out = (pltpu.HBM((8,) + PLANE, F32), HBM)
    y_out = (pltpu.HBM((8, S // 2, NYL), F32), HBM)
    halves_out = (pltpu.VMEM((2, S // 2, NYL), F32), VM)
    to_core = (jax.ShapeDtypeStruct((2, S // 2, NYL), F32), VM)
    pair_out = (pltpu.VMEM((2,) + PLANE, F32), VM)
    tables_out = (pltpu.VMEM((10,) + PLANE, F32), VM)
    result = (pltpu.HBM((S, NXL, NYL), F32), HBM)

    vectors = [(v.reshape(1, S), HBM) for v in (trophic_level, attack, disp_rate, disp_len)]
    b = (biomass, HBM)
    adj, cap = (adjacency, VM), (capacity, VM)
    cols, msg = call(
        tails_kernel,
        [b] + vectors,
        [plane_out, x_out],
        [field, pltpu.VMEM((1, S), jnp.int32), pltpu.VMEM((8, S), F32), x_sides[0], columns, pltpu.SemaphoreType.DMA((4,)), x_sides[1]],
        3,
    )
    cols = (in_vmem(cols), VM)
    rx = in_vmem(lax.all_to_all(msg, "gx", 0, 0))
    q, fun, tab = call(
        first_kernel,
        [b, adj, cap, cols],
        [field_out, plane_out, tables_out],
        [field, field, field, plane, columns, columns],
        12,
    )
    tab = (in_vmem(tab), VM)
    car, own, sides, msg = call(
        rows_kernel,
        [(rx, VM), (in_vmem(fun), VM), tab],
        [pair_out, plane_out, halves_out, y_out],
        [pltpu.SemaphoreType.DMA((8,))],
        1,
    )
    ry = in_vmem(lax.all_to_all(msg, "gy", 0, 0, axis_index_groups=same_core))
    mid, p, tail = call(
        local_kernel,
        [(q, HBM), (in_vmem(car), VM), cols],
        [field_out, field_out, pair_out],
        [field, field, plane, plane, columns, columns, columns],
        12,
    )
    part, msg = call(chips_kernel, [(ry, VM), (in_vmem(sides), VM), tab, (in_vmem(tail), VM)], [halves_out, to_core], [], 1)
    other = lax.ppermute(msg, "gy", other_core)
    coef, msg = call(
        columns_kernel, [(in_vmem(part), VM), (other, VM), (in_vmem(own), VM), (in_vmem(tail), VM), tab], [plane_out, x_out], x_sides, 1
    )
    rx = in_vmem(lax.all_to_all(msg, "gx", 0, 0))
    (part,) = call(
        second_kernel,
        [b, adj, cap, cols, tab, (mid, HBM), (p, HBM), (in_vmem(coef), VM)],
        [field_out],
        [field, field, field, plane, plane, columns, columns, columns, chunks],
        12,
    )
    (out,) = call(
        final_kernel, [(part, HBM), (rx, VM), cols, tab], [result], [plane, plane, field, columns, columns], 3
    )
    return out


def solution(mesh):
    return jax.shard_map(
        shards,
        mesh=mesh,
        in_specs=(P(None, "gx", "gy"), P("gx", "gy"), P(), P(), P(), P(), P()),
        out_specs=P(None, "gx", "gy"),
        check_vma=False,
    )
```

```python
import jax
import jax.numpy as jnp
from jax import lax
from jax.experimental import pallas as pl
from jax.experimental.pallas import tpu as pltpu
from jax.sharding import PartitionSpec as P

time_step = 0.25
handling = 1.0
efficiency = 0.6
mortal_rate = 0.15

S = 256
NXL = 32
NYL = 128
CH = 64
BX = 8
BR = 4
BL = 4
TURN_BY = 2
F32 = jnp.float32
BF16 = jnp.bfloat16
VMEM_LIMIT = 32 * 1024 * 1024


LAM, DEC, NORM2, RATE, ATT, BASAL, LEVEL = range(7)
HOP_X, HOP_Y, WF, FH, WB, BH, UP, DOWN, TURN, RUN = range(10)
GROUPS = (BH, WB, FH, WF)


def col(cols, k):
    return cols[:, k : k + 1]


def lanes(rows):
    return lax.broadcasted_iota(jnp.int32, (rows, NYL), 1)


def wide(column):
    return jnp.broadcast_to(column, (column.shape[0], NYL))


def lane_sum(v):
    return jnp.sum(v, axis=1, keepdims=True)


def split(v):
    hi = v.astype(BF16)
    lo = (v - hi.astype(F32)).astype(BF16)
    return jnp.concatenate([hi, lo], axis=1)


def triangles():
    i = lax.broadcasted_iota(jnp.int32, (2 * NYL, NYL), 0) % NYL
    j = lax.broadcasted_iota(jnp.int32, (2 * NYL, NYL), 1)
    return (i <= j).astype(F32).astype(BF16), (i > j).astype(F32).astype(BF16)


def smooth_rows(v, a, ia, low, upp):
    f = jnp.dot(split(v * ia), low, preferred_element_type=F32)
    g = jnp.dot(split(v * a), upp, preferred_element_type=F32)
    return f * a + g * ia


def smooth_and_total(v, a, ia, low, upp):
    f = jnp.dot(split(v * ia), low, preferred_element_type=F32)
    g = jnp.dot(split(v * a), upp, preferred_element_type=F32)
    return f[:, :NYL] * a + g[:, :NYL] * ia, f[:, NYL:], g[:, NYL:]


def respond(v, rcap, adj, adj_t, att, basal, level):
    p = jnp.maximum(v, 0.0)
    both = jnp.dot(adj_t, split(p), preferred_element_type=F32)
    grazing = att * (both[:, :NYL] + both[:, NYL:])
    handled = p / (1.0 + handling * grazing)
    back = jnp.dot(adj, split(att * handled), preferred_element_type=F32)
    loss = back[:, :NYL] + back[:, NYL:]
    return p * (basal - mortal_rate * level - basal * p * rcap - loss) + efficiency * handled * grazing


def food_web(adj_ref, cols):
    adj = adj_ref[...].astype(F32)
    return (adj.astype(BF16), adj.T.astype(BF16)) + tuple(wide(col(cols, k)) for k in (ATT, BASAL, LEVEL))


def read_carries(rx_ref, hop, me, count, slot):
    cf = jnp.zeros(rx_ref.shape[1:], F32)
    cb = jnp.zeros(rx_ref.shape[1:], F32)
    for k in range(count):
        cf = jnp.where(k < me, rx_ref[slot(k)] + hop * cf, cf)
    for k in range(count - 1, -1, -1):
        cb = jnp.where(k > me, rx_ref[slot(k)] + hop * cb, cb)
    return cf, cb


def column_slot(k):
    return (k + 8 - TURN_BY * (lax.axis_index("gy") % 2)) % 8


def send_messages(sides, msg_hbm, sems, me, count, slot):
    copies = [
        pltpu.make_async_copy(sides.at[(k > me).astype(jnp.int32)], msg_hbm.at[slot(k)], sems.at[k]) for k in range(count)
    ]
    for copy in copies:
        copy.start()
    for copy in copies:
        copy.wait()


def column_in(b_hbm, buf, sems, x):
    return pltpu.make_async_copy(b_hbm.at[:, x, :], buf.at[x], sems.at[x])


def plane_in(hbm, buf, sems, x):
    return pltpu.make_async_copy(hbm.at[x], buf.at[x], sems.at[x])


def plane_out(buf, hbm, sems, x):
    return pltpu.make_async_copy(buf.at[x], hbm.at[x], sems.at[x])


def chunk_out(buf, hbm, sems, i):
    part = pl.ds(pl.multiple_of(i * CH, CH), CH)
    return pltpu.make_async_copy(buf.at[:, part, :], hbm.at[:, part, :], sems.at[i])


def each(first, last, act):
    def body(k, _):
        act(k)
        return 0

    lax.fori_loop(first, last, body, 0)


def tails_kernel(b_hbm, level_hbm, attack_hbm, rate_hbm, length_hbm, cols_ref, msg_hbm, bt, level, vec, sides, sems, vsems, msems):
    sources = (length_hbm, rate_hbm, attack_hbm)
    small = [pltpu.make_async_copy(h, vec.at[pl.ds(k, 1), :], vsems.at[k]) for k, h in enumerate(sources)]
    small.append(pltpu.make_async_copy(level_hbm, level, vsems.at[3]))
    for copy in small:
        copy.start()
    copies = [column_in(b_hbm, bt, sems, x) for x in range(NXL)]
    for copy in copies:
        copy.start()
    for copy in small:
        copy.wait()
    me = lax.axis_index("gx")
    lam = 1.0 / vec[0:1, :]
    dec = jnp.exp(-lam)
    norm = (1.0 - dec) / (1.0 + dec)
    basal = (level[...] == 0).astype(F32)
    rows = [lam, dec, norm * norm, vec[1:2, :], vec[2:3, :], basal, level[...].astype(F32)]
    cols_ref[...] = jnp.concatenate(rows + [jnp.zeros((NYL - len(rows), S), F32)], axis=0).T
    for x0 in range(0, NXL, BX):
        for x in range(x0, x0 + BX):
            copies[x].wait()
        for s0 in range(0, S, CH):
            part = pl.ds(s0, CH)
            d = wide(cols_ref[part, DEC : DEC + 1])
            vs = [bt[x, part, :] for x in range(x0, x0 + BX)]
            f = sides[1, part, :] if x0 else jnp.zeros((CH, NYL), F32)
            for v in vs:
                f = v + d * f
            g = vs[-1]
            for v in vs[-2::-1]:
                g = v + d * g
            if x0:
                g = sides[0, part, :] + wide(jnp.exp(-float(x0) * cols_ref[part, LAM : LAM + 1])) * g
            sides[1, part, :] = f
            sides[0, part, :] = g
    send_messages(sides, msg_hbm, msems, me, 8, column_slot)


def by_group(lane, parts):
    out = parts[3]
    for k in (2, 1, 0):
        out = jnp.where(lane < 32 * (k + 1), parts[k], out)
    return out


def fill_tables(tab_ref, cols, my):
    lam, dec = col(cols, LAM), col(cols, DEC)
    c = time_step * col(cols, RATE) * col(cols, NORM2)
    lane = lanes(S)
    y = lane.astype(F32)
    xl = (lane % 32).astype(F32)
    inv = 1.0 / ((1.0 - dec) * (1.0 + dec))
    wf = jnp.exp(-lam * (127.0 - y))
    wb = jnp.exp(-lam * y)
    tab_ref[HOP_X] = wide(jnp.exp(-32.0 * lam))
    tab_ref[HOP_Y] = wide(jnp.exp(-128.0 * lam))
    tab_ref[WF] = wf
    tab_ref[WB] = wb
    tab_ref[FH] = c * ((128.0 - y) * wf + (jnp.exp(-lam * (129.0 - y)) - jnp.exp(-lam * (129.0 + y))) * inv)
    tab_ref[BH] = c * ((y + 1.0) * wb + (jnp.exp(-lam * (y + 2.0)) - jnp.exp(-lam * (256.0 - y))) * inv)
    tab_ref[UP] = jnp.exp(-lam * (xl + 1.0))
    tab_ref[DOWN] = jnp.exp(-lam * (32.0 - xl))
    below, above = my.astype(F32), (15 - my).astype(F32)
    scale = c * dec * inv
    zero = jnp.zeros((S, 1), F32)
    tb = scale * (1.0 - jnp.exp(-256.0 * below * lam))
    ta = scale * (1.0 - jnp.exp(-256.0 * above * lam))
    tab_ref[TURN] = by_group(lane, [zero, tb, zero, ta])
    run = 128.0 * c
    tab_ref[RUN] = by_group(lane, [zero, run, zero, run])


def first_kernel(
    b_hbm, adj_ref, cap_ref, cols_ref, q_hbm, fun_ref, tab_ref, bt_ref, q_ref, u_ref, f_ref, b_sems, q_sems
):
    each(0, NXL, lambda x: column_in(b_hbm, bt_ref, b_sems, x).start())
    cols = cols_ref[...]
    fill_tables(tab_ref, cols, lax.axis_index("gy"))
    web = food_web(adj_ref, cols)
    rate, d = wide(col(cols, RATE)), wide(col(cols, DEC))
    f_ref[...] = jnp.zeros_like(f_ref)

    def response(i, _):
        for j in range(BR):
            x = i * BR + j
            column_in(b_hbm, bt_ref, b_sems, x).wait()
        for j in range(BR):
            x = i * BR + j
            v = bt_ref[x]
            rcap = 1.0 / cap_ref[pl.ds(x, 1), :]
            q_ref[x] = v + time_step * (respond(v, rcap, *web) - rate * v)
            f = v + d * f_ref[...]
            f_ref[...] = f
            u_ref[x] = f
        return 0

    lax.fori_loop(0, NXL // BR, response, 0)

    low, upp = triangles()
    ones = jnp.ones((2 * NYL, NYL), BF16)
    low, upp = jnp.concatenate([low, ones], axis=1), jnp.concatenate([upp, ones], axis=1)
    lam = col(cols, LAM)
    c = wide(time_step * col(cols, RATE) * col(cols, NORM2))
    lane = lanes(S)
    y = lane.astype(F32) - 64.0
    a, ia = jnp.exp(-lam * y), jnp.exp(lam * y)
    f_ref[...] = jnp.zeros_like(f_ref)
    fun_ref[...] = jnp.zeros_like(fun_ref)

    def smoothing(i, _):
        for j in range(BL):
            x = NXL - 1 - (i * BL + j)
            g = d * f_ref[...]
            u = u_ref[x] + g
            f_ref[...] = g + bt_ref[x]
            smooth, total_f, total_b = smooth_and_total(u, a, ia, low, upp)
            q = q_ref[x] + c * smooth
            q_ref[x] = q
            acc = jnp.where(lane == x, total_f, fun_ref[...])
            acc = jnp.where(lane == x + 32, lane_sum(tab_ref[WF] * q), acc)
            acc = jnp.where(lane == x + 64, total_b, acc)
            fun_ref[...] = jnp.where(lane == x + 96, lane_sum(tab_ref[WB] * q), acc)
        for j in range(BL):
            plane_out(q_ref, q_hbm, q_sems, NXL - 1 - (i * BL + j)).start()
        return 0

    lax.fori_loop(0, NXL // BL, smoothing, 0)
    one = jnp.ones_like(lam)
    fun_ref[...] = fun_ref[...] * by_group(lane, [jnp.exp(-63.0 * lam), one, jnp.exp(-64.0 * lam), one])
    each(0, NXL, lambda x: plane_out(q_ref, q_hbm, q_sems, x).wait())


def rows_kernel(rx_ref, fun_ref, tab_ref, car_ref, own_ref, sides, msg_hbm, msems):
    mx, my = lax.axis_index("gx"), lax.axis_index("gy")
    cf, cb = read_carries(rx_ref, tab_ref[HOP_X], mx, 8, column_slot)
    car_ref[0] = cf
    car_ref[1] = cb
    lane = lanes(S)
    pf = by_group(lane, [lane_sum(tab_ref[k] * cf) for k in (WF, FH, WB, BH)])
    pb = by_group(lane, [lane_sum(tab_ref[k] * cb) for k in (WF, FH, WB, BH)])
    fun = fun_ref[...] + tab_ref[UP] * pf + tab_ref[DOWN] * pb
    own_ref[...] = fun
    fun = fun + tab_ref[TURN] * tab_ref[HOP_Y] * pltpu.roll(fun, 96, 1)
    half = S // 2
    low_lanes = lanes(half) < 64
    sides[1] = jnp.where(low_lanes, fun[:half], pltpu.roll(fun[half:], 64, 1))
    sides[0] = jnp.where(low_lanes, pltpu.roll(fun[:half], 64, 1), fun[half:])
    send_messages(sides, msg_hbm, msems, my // 2, 8, lambda k: k)


def local_kernel(
    q_hbm, car_ref, cols_ref, mid_hbm, p_hbm, tail_ref, q_ref, p_ref, up_ref, down_ref, q_sems, p_sems, m_sems
):
    each(0, NXL, lambda x: plane_in(q_hbm, q_ref, q_sems, x).start())
    cols = cols_ref[...]
    lam = col(cols, LAM)
    c = wide(time_step * col(cols, RATE) * col(cols, NORM2))
    d = wide(col(cols, DEC))
    inv_d = wide(jnp.exp(lam))
    y = lanes(S).astype(F32) - 64.0
    a, ia = jnp.exp(-lam * y), jnp.exp(lam * y)
    low, upp = triangles()
    tail_ref[...] = jnp.zeros_like(tail_ref)
    up_ref[...] = c * d * smooth_rows(car_ref[0], a, ia, low, upp)
    down_ref[...] = c * jnp.exp(-32.0 * lam) * smooth_rows(car_ref[1], a, ia, low, upp)

    def step(i, weight):
        for j in range(BL):
            plane_in(q_hbm, q_ref, q_sems, i * BL + j).wait()
        for j in range(BL):
            x = i * BL + j
            up, down = up_ref[...], down_ref[...]
            mid = q_ref[x] + up + down
            q_ref[x] = mid
            p = smooth_rows(mid, a, ia, low, upp)
            p_ref[x] = p
            tail_ref[0] = p + d * tail_ref[0]
            tail_ref[1] = tail_ref[1] + weight * p
            up_ref[...] = up * d
            down_ref[...] = down * inv_d
            weight = weight * col(cols, DEC)
        for j in range(BL):
            plane_out(q_ref, mid_hbm, m_sems, i * BL + j).start()
            plane_out(p_ref, p_hbm, p_sems, i * BL + j).start()
        return weight

    lax.fori_loop(0, NXL // BL, step, jnp.ones((S, 1), F32))

    def drain(x):
        plane_out(q_ref, mid_hbm, m_sems, x).wait()
        plane_out(p_ref, p_hbm, p_sems, x).wait()

    each(0, NXL, drain)


def packed(low_lanes, v):
    return jnp.where(low_lanes, v[: S // 2], v[S // 2 :])


def chips_kernel(ry_ref, sides_ref, tab_ref, tail_ref, part_ref, msg_ref):
    my = lax.axis_index("gy")
    del tail_ref
    chip, core = my // 2, my % 2
    half = S // 2
    low_lanes = lanes(half) < 64
    hop = packed(low_lanes, tab_ref[HOP_Y])
    run = packed(low_lanes, tab_ref[RUN])
    hop2 = hop * hop
    zero = jnp.zeros((half, NYL), F32)
    lo, lo2, hi, hi2 = zero, zero, zero, zero
    for k in range(7):
        lo2 = jnp.where(k < chip, hop2 * (lo2 + lo), lo2)
        lo = jnp.where(k < chip, ry_ref[k] + hop2 * lo, lo)
    for k in range(7, 0, -1):
        hi2 = jnp.where(k > chip, hop2 * (hi2 + hi), hi2)
        hi = jnp.where(k > chip, ry_ref[k] + hop2 * hi, hi)

    def same(z, z2):
        return hop * z + run * pltpu.roll(hop * (2.0 * z2 + z), 32, 1)

    def near(z, z2):
        return z + run * pltpu.roll(2.0 * z2, 32, 1)

    def far(z, z2):
        return hop2 * z + run * pltpu.roll(2.0 * hop2 * (z2 + z), 32, 1)

    part_ref[0] = same(lo, lo2)
    part_ref[1] = same(hi, hi2)
    msg_ref[0] = jnp.where(core == 0, far(lo, lo2) + sides_ref[1], near(lo, lo2))
    msg_ref[1] = jnp.where(core == 1, far(hi, hi2) + sides_ref[0], near(hi, hi2))


def columns_kernel(part_ref, other_ref, own_ref, tail_ref, tab_ref, coef_ref, msg_hbm, sides, msems):
    mx = lax.axis_index("gx")
    low_lanes = lanes(S // 2) < 64
    lo = part_ref[0] + other_ref[0]
    hi = part_ref[1] + other_ref[1]
    top = jnp.where(low_lanes, lo, pltpu.roll(hi, 64, 1))
    bottom = jnp.where(low_lanes, pltpu.roll(lo, 64, 1), hi)
    coef = jnp.concatenate([top, bottom], axis=0)
    coef = coef + tab_ref[TURN] * pltpu.roll(own_ref[...] + tab_ref[HOP_Y] * coef, 96, 1)
    coef_ref[...] = coef
    lane = lanes(S)
    at_front, at_back = coef * tab_ref[DOWN], coef * tab_ref[UP]
    front, back = tail_ref[0], tail_ref[1]
    for k, table in enumerate(GROUPS):
        inside = (lane >= 32 * k) & (lane < 32 * (k + 1))
        weight = tab_ref[table]
        front = front + lane_sum(jnp.where(inside, at_front, 0.0)) * weight
        back = back + lane_sum(jnp.where(inside, at_back, 0.0)) * weight
    sides[1] = front
    sides[0] = back
    send_messages(sides, msg_hbm, msems, mx, 8, column_slot)


def second_kernel(
    b_hbm, adj_ref, cap_ref, cols_ref, tab_ref, mid_hbm, p_hbm, coef_ref, out_hbm,
    out_ref, mid_ref, v_ref, roll_ref, f_ref, b_sems, m_sems, p_sems, o_sems,
):
    def fetch(x):
        column_in(b_hbm, out_ref, b_sems, x).start()
        plane_in(mid_hbm, mid_ref, m_sems, x).start()
        plane_in(p_hbm, v_ref, p_sems, x).start()

    each(0, NXL, fetch)
    cols = cols_ref[...]
    web = food_web(adj_ref, cols)
    rate, d = wide(col(cols, RATE)), wide(col(cols, DEC))
    c = wide(time_step * col(cols, RATE) * col(cols, NORM2))
    ef, eb, alpha, beta = (d * tab_ref[k] for k in (WB, WF, BH, FH))
    e = wide(0.5 * time_step * col(cols, RATE) * col(cols, NORM2))
    roll_ref[...] = coef_ref[...]
    f_ref[...] = jnp.zeros_like(f_ref)

    def response(i, _):
        for j in range(BR):
            x = i * BR + j
            column_in(b_hbm, out_ref, b_sems, x).wait()
            plane_in(mid_hbm, mid_ref, m_sems, x).wait()
            plane_in(p_hbm, v_ref, p_sems, x).wait()
        for j in range(BR):
            x = i * BR + j
            coef = roll_ref[...]
            cfu, cfm, cbu, cbm = (coef[:, 32 * k : 32 * k + 1] for k in range(4))
            roll_ref[...] = pltpu.roll(coef, 127, 1)
            mid = mid_ref[x] + c * (cfu * ef + cbu * eb)
            v = v_ref[x] + cfu * alpha + cbu * beta + cfm * ef + cbm * eb
            v_ref[x] = v
            f = v + d * f_ref[...]
            f_ref[...] = f
            rcap = 1.0 / cap_ref[pl.ds(x, 1), :]
            r = respond(mid, rcap, *web)
            out_ref[x] = 0.5 * (out_ref[x] + mid) + 0.5 * time_step * (r - rate * mid) + e * f
        return 0

    lax.fori_loop(0, NXL // BR, response, 0)

    def chunk(i, _):
        part = pl.ds(pl.multiple_of(i * CH, CH), CH)
        d = wide(cols_ref[part, DEC : DEC + 1])
        e = wide(0.5 * time_step * cols_ref[part, RATE : RATE + 1] * cols_ref[part, NORM2 : NORM2 + 1])

        def bwd(k, g):
            for j in range(BX):
                x = NXL - 1 - (k * BX + j)
                g = d * g
                out_ref[x, part, :] = out_ref[x, part, :] + e * g
                g = g + v_ref[x, part, :]
            return g

        lax.fori_loop(0, NXL // BX, bwd, jnp.zeros((CH, NYL), F32))
        chunk_out(out_ref, out_hbm, o_sems, i).start()
        return 0

    lax.fori_loop(0, S // CH, chunk, 0)
    each(0, S // CH, lambda i: chunk_out(out_ref, out_hbm, o_sems, i).wait())


def final_kernel(o_hbm, rx_ref, cols_ref, tab_ref, out_hbm, cf_ref, cb_ref, buf, in_sems, sems):
    loads = [plane_in(o_hbm, buf, in_sems, x) for x in range(NXL)]
    for copy in loads:
        copy.start()
    cols = cols_ref[...]
    lam = col(cols, LAM)
    e = 0.5 * time_step * col(cols, RATE) * col(cols, NORM2)
    cf, cb = read_carries(rx_ref, tab_ref[HOP_X], lax.axis_index("gx"), 8, column_slot)
    cf_ref[...] = cf * (e * col(cols, DEC))
    cb_ref[...] = cb * (e * jnp.exp(-32.0 * lam))
    copies = [pltpu.make_async_copy(buf.at[x], out_hbm.at[:, x, :], sems.at[x]) for x in range(NXL)]
    for x0 in range(0, NXL, BX):
        for x in range(x0, x0 + BX):
            loads[x].wait()
        for s0 in range(0, S, CH):
            part = pl.ds(s0, CH)
            d = wide(cols_ref[part, DEC : DEC + 1])
            inv_d = wide(jnp.exp(cols_ref[part, LAM : LAM + 1]))
            f, g = cf_ref[part, :], cb_ref[part, :]
            for x in range(x0, x0 + BX):
                buf[x, part, :] = buf[x, part, :] + f + g
                f = f * d
                g = g * inv_d
            cf_ref[part, :] = f
            cb_ref[part, :] = g
        for x in range(x0, x0 + BX):
            copies[x].start()
    for copy in copies:
        copy.wait()


VM = pl.BlockSpec(memory_space=pltpu.VMEM)
HBM = pl.BlockSpec(memory_space=pltpu.HBM)
FIELD = (NXL, S, NYL)
PLANE = (S, NYL)


def in_vmem(x):
    return pltpu.with_memory_space_constraint(x, pltpu.VMEM)


def in_hbm(x):
    return pltpu.with_memory_space_constraint(x, pltpu.HBM)


def call(kernel, operands, outs, scratch, microseconds):
    cost = pl.CostEstimate(flops=int(microseconds * 1e9), bytes_accessed=int(microseconds * 2e6), transcendentals=0)
    return pl.pallas_call(
        kernel,
        out_shape=[shape for shape, _ in outs],
        in_specs=[spec for _, spec in operands],
        out_specs=[spec for _, spec in outs],
        scratch_shapes=scratch,
        cost_estimate=cost,
        compiler_params=pltpu.CompilerParams(vmem_limit_bytes=VMEM_LIMIT),
    )(*[in_hbm(x) if spec is HBM else x for x, spec in operands])


def shards(biomass, capacity, adjacency, trophic_level, attack, disp_rate, disp_len):
    field = pltpu.VMEM(FIELD, F32)
    plane = pltpu.VMEM(PLANE, F32)
    columns = pltpu.SemaphoreType.DMA((NXL,))
    chunks = pltpu.SemaphoreType.DMA((S // CH,))
    x_sides = [pltpu.VMEM((2,) + PLANE, F32), pltpu.SemaphoreType.DMA((8,))]
    same_row = [[(k + TURN_BY * (row % 2)) % 8 * 16 + row for k in range(8)] for row in range(16)]
    same_core = [[core + 2 * chip for chip in range(8)] for core in range(2)]
    other_core = [(k, k ^ 1) for k in range(16)]
    field_out = (pltpu.HBM(FIELD, F32), HBM)
    plane_out = (plane, VM)
    x_out = (pltpu.HBM((8,) + PLANE, F32), HBM)
    y_out = (pltpu.HBM((8, S // 2, NYL), F32), HBM)
    halves_out = (pltpu.VMEM((2, S // 2, NYL), F32), VM)
    to_core = (jax.ShapeDtypeStruct((2, S // 2, NYL), F32), VM)
    pair_out = (pltpu.VMEM((2,) + PLANE, F32), VM)
    tables_out = (pltpu.VMEM((10,) + PLANE, F32), VM)
    result = (pltpu.HBM((S, NXL, NYL), F32), HBM)

    vectors = [(v.reshape(1, S), HBM) for v in (trophic_level, attack, disp_rate, disp_len)]
    b = (biomass, HBM)
    adj, cap = (adjacency, VM), (capacity, VM)
    cols, msg = call(
        tails_kernel,
        [b] + vectors,
        [plane_out, x_out],
        [field, pltpu.VMEM((1, S), jnp.int32), pltpu.VMEM((8, S), F32), x_sides[0], columns, pltpu.SemaphoreType.DMA((4,)), x_sides[1]],
        3,
    )
    cols = (in_vmem(cols), VM)
    rx = in_vmem(lax.all_to_all(msg, ("gx", "gy"), 0, 0, axis_index_groups=same_row))
    q, fun, tab = call(
        first_kernel,
        [b, adj, cap, cols],
        [field_out, plane_out, tables_out],
        [field, field, field, plane, columns, columns],
        12,
    )
    tab = (in_vmem(tab), VM)
    car, own, sides, msg = call(
        rows_kernel,
        [(rx, VM), (in_vmem(fun), VM), tab],
        [pair_out, plane_out, halves_out, y_out],
        [pltpu.SemaphoreType.DMA((8,))],
        1,
    )
    ry = in_vmem(lax.all_to_all(msg, "gy", 0, 0, axis_index_groups=same_core))
    mid, p, tail = call(
        local_kernel,
        [(q, HBM), (in_vmem(car), VM), cols],
        [field_out, field_out, pair_out],
        [field, field, plane, plane, columns, columns, columns],
        12,
    )
    part, msg = call(chips_kernel, [(ry, VM), (in_vmem(sides), VM), tab, (in_vmem(tail), VM)], [halves_out, to_core], [], 1)
    other = lax.ppermute(msg, "gy", other_core)
    coef, msg = call(
        columns_kernel, [(in_vmem(part), VM), (other, VM), (in_vmem(own), VM), (in_vmem(tail), VM), tab], [plane_out, x_out], x_sides, 1
    )
    rx = in_vmem(lax.all_to_all(msg, ("gx", "gy"), 0, 0, axis_index_groups=same_row))
    (part,) = call(
        second_kernel,
        [b, adj, cap, cols, tab, (mid, HBM), (p, HBM), (in_vmem(coef), VM)],
        [field_out],
        [field, field, field, plane, plane, columns, columns, columns, chunks],
        12,
    )
    (out,) = call(
        final_kernel, [(part, HBM), (rx, VM), cols, tab], [result], [plane, plane, field, columns, columns], 3
    )
    return out


def solution(mesh):
    return jax.shard_map(
        shards,
        mesh=mesh,
        in_specs=(P(None, "gx", "gy"), P("gx", "gy"), P(), P(), P(), P(), P()),
        out_specs=P(None, "gx", "gy"),
        check_vma=False,
    )
```

```python
import jax
import jax.numpy as jnp
from jax import lax
from jax.experimental import pallas as pl
from jax.experimental.pallas import tpu as pltpu
from jax.sharding import PartitionSpec as P

time_step = 0.25
handling = 1.0
efficiency = 0.6
mortal_rate = 0.15

S = 256
NXL = 32
NYL = 128
CH = 64
BX = 8
BR = 4
BL = 4
TURN_BY = 2
F32 = jnp.float32
BF16 = jnp.bfloat16
VMEM_LIMIT = 32 * 1024 * 1024


LAM, DEC, NORM2, RATE, ATT, BASAL, LEVEL = range(7)
HOP_X, HOP_Y, WF, FH, WB, BH, UP, DOWN, TURN, RUN = range(10)
GROUPS = (BH, WB, FH, WF)


def col(cols, k):
    return cols[:, k : k + 1]


def lanes(rows):
    return lax.broadcasted_iota(jnp.int32, (rows, NYL), 1)


def wide(column):
    return jnp.broadcast_to(column, (column.shape[0], NYL))


def lane_sum(v):
    return jnp.sum(v, axis=1, keepdims=True)


def split(v):
    hi = v.astype(BF16)
    lo = (v - hi.astype(F32)).astype(BF16)
    return jnp.concatenate([hi, lo], axis=1)


def triangles():
    i = lax.broadcasted_iota(jnp.int32, (2 * NYL, NYL), 0) % NYL
    j = lax.broadcasted_iota(jnp.int32, (2 * NYL, NYL), 1)
    return (i <= j).astype(F32).astype(BF16), (i > j).astype(F32).astype(BF16)


def smooth_rows(v, a, ia, low, upp):
    f = jnp.dot(split(v * ia), low, preferred_element_type=F32)
    g = jnp.dot(split(v * a), upp, preferred_element_type=F32)
    return f * a + g * ia


def smooth_and_total(v, a, ia, low, upp):
    f = jnp.dot(split(v * ia), low, preferred_element_type=F32)
    g = jnp.dot(split(v * a), upp, preferred_element_type=F32)
    return f[:, :NYL] * a + g[:, :NYL] * ia, f[:, NYL:], g[:, NYL:]


def respond(v, rcap, adj, adj_t, att, basal, level):
    p = jnp.maximum(v, 0.0)
    both = jnp.dot(adj_t, split(p), preferred_element_type=F32)
    grazing = att * (both[:, :NYL] + both[:, NYL:])
    handled = p / (1.0 + handling * grazing)
    back = jnp.dot(adj, split(att * handled), preferred_element_type=F32)
    loss = back[:, :NYL] + back[:, NYL:]
    return p * (basal - mortal_rate * level - basal * p * rcap - loss) + efficiency * handled * grazing


def food_web(adj_ref, cols):
    adj = adj_ref[...].astype(F32)
    return (adj.astype(BF16), adj.T.astype(BF16)) + tuple(wide(col(cols, k)) for k in (ATT, BASAL, LEVEL))


def read_carries(rx_ref, hop, me, count, slot):
    cf = jnp.zeros(rx_ref.shape[1:], F32)
    cb = jnp.zeros(rx_ref.shape[1:], F32)
    for k in range(count):
        cf = jnp.where(k < me, rx_ref[slot(k)] + hop * cf, cf)
    for k in range(count - 1, -1, -1):
        cb = jnp.where(k > me, rx_ref[slot(k)] + hop * cb, cb)
    return cf, cb


def column_slot(k):
    return (k + 8 - TURN_BY * (lax.axis_index("gy") % 2)) % 8


def send_messages(sides, msg_hbm, sems, me, count, slot):
    copies = [
        pltpu.make_async_copy(sides.at[(k > me).astype(jnp.int32)], msg_hbm.at[slot(k)], sems.at[k]) for k in range(count)
    ]
    for copy in copies:
        copy.start()
    for copy in copies:
        copy.wait()


def column_in(b_hbm, buf, sems, x):
    return pltpu.make_async_copy(b_hbm.at[:, x, :], buf.at[x], sems.at[x])


def plane_in(hbm, buf, sems, x):
    return pltpu.make_async_copy(hbm.at[x], buf.at[x], sems.at[x])


def plane_out(buf, hbm, sems, x):
    return pltpu.make_async_copy(buf.at[x], hbm.at[x], sems.at[x])


def chunk_out(buf, hbm, sems, i):
    part = pl.ds(pl.multiple_of(i * CH, CH), CH)
    return pltpu.make_async_copy(buf.at[:, part, :], hbm.at[:, part, :], sems.at[i])


def each(first, last, act):
    def body(k, _):
        act(k)
        return 0

    lax.fori_loop(first, last, body, 0)


def tails_kernel(b_hbm, level_hbm, attack_hbm, rate_hbm, length_hbm, cols_ref, msg_hbm, bt, level, vec, sides, sems, vsems, msems):
    sources = (length_hbm, rate_hbm, attack_hbm)
    small = [pltpu.make_async_copy(h, vec.at[pl.ds(k, 1), :], vsems.at[k]) for k, h in enumerate(sources)]
    small.append(pltpu.make_async_copy(level_hbm, level, vsems.at[3]))
    for copy in small:
        copy.start()
    copies = [column_in(b_hbm, bt, sems, x) for x in range(NXL)]
    for copy in copies:
        copy.start()
    for copy in small:
        copy.wait()
    me = lax.axis_index("gx")
    lam = 1.0 / vec[0:1, :]
    dec = jnp.exp(-lam)
    norm = (1.0 - dec) / (1.0 + dec)
    basal = (level[...] == 0).astype(F32)
    rows = [lam, dec, norm * norm, vec[1:2, :], vec[2:3, :], basal, level[...].astype(F32)]
    cols_ref[...] = jnp.concatenate(rows + [jnp.zeros((NYL - len(rows), S), F32)], axis=0).T
    for x0 in range(0, NXL, BX):
        for x in range(x0, x0 + BX):
            copies[x].wait()
        for s0 in range(0, S, CH):
            part = pl.ds(s0, CH)
            d = wide(cols_ref[part, DEC : DEC + 1])
            vs = [bt[x, part, :] for x in range(x0, x0 + BX)]
            f = sides[1, part, :] if x0 else jnp.zeros((CH, NYL), F32)
            for v in vs:
                f = v + d * f
            g = vs[-1]
            for v in vs[-2::-1]:
                g = v + d * g
            if x0:
                g = sides[0, part, :] + wide(jnp.exp(-float(x0) * cols_ref[part, LAM : LAM + 1])) * g
            sides[1, part, :] = f
            sides[0, part, :] = g
    send_messages(sides, msg_hbm, msems, me, 8, column_slot)


def by_group(lane, parts):
    out = parts[3]
    for k in (2, 1, 0):
        out = jnp.where(lane < 32 * (k + 1), parts[k], out)
    return out


def fill_tables(tab_ref, cols, my):
    lam, dec = col(cols, LAM), col(cols, DEC)
    c = time_step * col(cols, RATE) * col(cols, NORM2)
    lane = lanes(S)
    y = lane.astype(F32)
    xl = (lane % 32).astype(F32)
    inv = 1.0 / ((1.0 - dec) * (1.0 + dec))
    wf = jnp.exp(-lam * (127.0 - y))
    wb = jnp.exp(-lam * y)
    tab_ref[HOP_X] = wide(jnp.exp(-32.0 * lam))
    tab_ref[HOP_Y] = wide(jnp.exp(-128.0 * lam))
    tab_ref[WF] = wf
    tab_ref[WB] = wb
    tab_ref[FH] = c * ((128.0 - y) * wf + (jnp.exp(-lam * (129.0 - y)) - jnp.exp(-lam * (129.0 + y))) * inv)
    tab_ref[BH] = c * ((y + 1.0) * wb + (jnp.exp(-lam * (y + 2.0)) - jnp.exp(-lam * (256.0 - y))) * inv)
    tab_ref[UP] = jnp.exp(-lam * (xl + 1.0))
    tab_ref[DOWN] = jnp.exp(-lam * (32.0 - xl))
    below, above = my.astype(F32), (15 - my).astype(F32)
    scale = c * dec * inv
    zero = jnp.zeros((S, 1), F32)
    tb = scale * (1.0 - jnp.exp(-256.0 * below * lam))
    ta = scale * (1.0 - jnp.exp(-256.0 * above * lam))
    tab_ref[TURN] = by_group(lane, [zero, tb, zero, ta])
    run = 128.0 * c
    tab_ref[RUN] = by_group(lane, [zero, run, zero, run])


def first_kernel(
    b_hbm, adj_ref, cap_ref, cols_ref, q_hbm, fun_ref, tab_ref, bt_ref, q_ref, u_ref, f_ref, b_sems, q_sems
):
    each(0, NXL, lambda x: column_in(b_hbm, bt_ref, b_sems, x).start())
    cols = cols_ref[...]
    fill_tables(tab_ref, cols, lax.axis_index("gy"))
    web = food_web(adj_ref, cols)
    rate, d = wide(col(cols, RATE)), wide(col(cols, DEC))
    f_ref[...] = jnp.zeros_like(f_ref)

    def response(i, _):
        for j in range(BR):
            x = i * BR + j
            column_in(b_hbm, bt_ref, b_sems, x).wait()
        for j in range(BR):
            x = i * BR + j
            v = bt_ref[x]
            rcap = 1.0 / cap_ref[pl.ds(x, 1), :]
            q_ref[x] = v + time_step * (respond(v, rcap, *web) - rate * v)
            f = v + d * f_ref[...]
            f_ref[...] = f
            u_ref[x] = f
        return 0

    lax.fori_loop(0, NXL // BR, response, 0)

    low, upp = triangles()
    ones = jnp.ones((2 * NYL, NYL), BF16)
    low, upp = jnp.concatenate([low, ones], axis=1), jnp.concatenate([upp, ones], axis=1)
    lam = col(cols, LAM)
    c = wide(time_step * col(cols, RATE) * col(cols, NORM2))
    lane = lanes(S)
    y = lane.astype(F32) - 64.0
    a, ia = jnp.exp(-lam * y), jnp.exp(lam * y)
    f_ref[...] = jnp.zeros_like(f_ref)
    fun_ref[...] = jnp.zeros_like(fun_ref)

    def smoothing(i, _):
        for j in range(BL):
            x = NXL - 1 - (i * BL + j)
            g = d * f_ref[...]
            u = u_ref[x] + g
            f_ref[...] = g + bt_ref[x]
            smooth, total_f, total_b = smooth_and_total(u, a, ia, low, upp)
            q = q_ref[x] + c * smooth
            q_ref[x] = q
            acc = jnp.where(lane == x, total_f, fun_ref[...])
            acc = jnp.where(lane == x + 32, lane_sum(tab_ref[WF] * q), acc)
            acc = jnp.where(lane == x + 64, total_b, acc)
            fun_ref[...] = jnp.where(lane == x + 96, lane_sum(tab_ref[WB] * q), acc)
        for j in range(BL):
            plane_out(q_ref, q_hbm, q_sems, NXL - 1 - (i * BL + j)).start()
        return 0

    lax.fori_loop(0, NXL // BL, smoothing, 0)
    one = jnp.ones_like(lam)
    fun_ref[...] = fun_ref[...] * by_group(lane, [jnp.exp(-63.0 * lam), one, jnp.exp(-64.0 * lam), one])
    each(0, NXL, lambda x: plane_out(q_ref, q_hbm, q_sems, x).wait())


def rows_kernel(rx_ref, fun_ref, tab_ref, car_ref, own_ref, sides, msg_hbm, msems):
    mx, my = lax.axis_index("gx"), lax.axis_index("gy")
    cf, cb = read_carries(rx_ref, tab_ref[HOP_X], mx, 8, column_slot)
    car_ref[0] = cf
    car_ref[1] = cb
    lane = lanes(S)
    pf = by_group(lane, [lane_sum(tab_ref[k] * cf) for k in (WF, FH, WB, BH)])
    pb = by_group(lane, [lane_sum(tab_ref[k] * cb) for k in (WF, FH, WB, BH)])
    fun = fun_ref[...] + tab_ref[UP] * pf + tab_ref[DOWN] * pb
    own_ref[...] = fun
    fun = fun + tab_ref[TURN] * tab_ref[HOP_Y] * pltpu.roll(fun, 96, 1)
    half = S // 2
    low_lanes = lanes(half) < 64
    sides[1] = jnp.where(low_lanes, fun[:half], pltpu.roll(fun[half:], 64, 1))
    sides[0] = jnp.where(low_lanes, pltpu.roll(fun[:half], 64, 1), fun[half:])
    send_messages(sides, msg_hbm, msems, my // 2, 8, lambda k: k)


def local_kernel(
    q_hbm, car_ref, cols_ref, mid_hbm, p_hbm, tail_ref, q_ref, p_ref, up_ref, down_ref, q_sems, p_sems, m_sems
):
    each(0, NXL, lambda x: plane_in(q_hbm, q_ref, q_sems, x).start())
    cols = cols_ref[...]
    lam = col(cols, LAM)
    c = wide(time_step * col(cols, RATE) * col(cols, NORM2))
    d = wide(col(cols, DEC))
    inv_d = wide(jnp.exp(lam))
    y = lanes(S).astype(F32) - 64.0
    a, ia = jnp.exp(-lam * y), jnp.exp(lam * y)
    low, upp = triangles()
    tail_ref[...] = jnp.zeros_like(tail_ref)
    up_ref[...] = c * d * smooth_rows(car_ref[0], a, ia, low, upp)
    down_ref[...] = c * jnp.exp(-32.0 * lam) * smooth_rows(car_ref[1], a, ia, low, upp)

    def step(i, weight):
        for j in range(BL):
            plane_in(q_hbm, q_ref, q_sems, i * BL + j).wait()
        for j in range(BL):
            x = i * BL + j
            up, down = up_ref[...], down_ref[...]
            mid = q_ref[x] + up + down
            q_ref[x] = mid
            p = smooth_rows(mid, a, ia, low, upp)
            p_ref[x] = p
            tail_ref[0] = p + d * tail_ref[0]
            tail_ref[1] = tail_ref[1] + weight * p
            up_ref[...] = up * d
            down_ref[...] = down * inv_d
            weight = weight * col(cols, DEC)
        for j in range(BL):
            plane_out(q_ref, mid_hbm, m_sems, i * BL + j).start()
            plane_out(p_ref, p_hbm, p_sems, i * BL + j).start()
        return weight

    lax.fori_loop(0, NXL // BL, step, jnp.ones((S, 1), F32))

    def drain(x):
        plane_out(q_ref, mid_hbm, m_sems, x).wait()
        plane_out(p_ref, p_hbm, p_sems, x).wait()

    each(0, NXL, drain)


def packed(low_lanes, v):
    return jnp.where(low_lanes, v[: S // 2], v[S // 2 :])


def chips_kernel(ry_ref, sides_ref, tab_ref, tail_ref, part_ref, msg_ref):
    my = lax.axis_index("gy")
    del tail_ref
    chip, core = my // 2, my % 2
    half = S // 2
    low_lanes = lanes(half) < 64
    hop = packed(low_lanes, tab_ref[HOP_Y])
    run = packed(low_lanes, tab_ref[RUN])
    hop2 = hop * hop
    zero = jnp.zeros((half, NYL), F32)
    lo, lo2, hi, hi2 = zero, zero, zero, zero
    for k in range(7):
        lo2 = jnp.where(k < chip, hop2 * (lo2 + lo), lo2)
        lo = jnp.where(k < chip, ry_ref[k] + hop2 * lo, lo)
    for k in range(7, 0, -1):
        hi2 = jnp.where(k > chip, hop2 * (hi2 + hi), hi2)
        hi = jnp.where(k > chip, ry_ref[k] + hop2 * hi, hi)

    def same(z, z2):
        return hop * z + run * pltpu.roll(hop * (2.0 * z2 + z), 32, 1)

    def near(z, z2):
        return z + run * pltpu.roll(2.0 * z2, 32, 1)

    def far(z, z2):
        return hop2 * z + run * pltpu.roll(2.0 * hop2 * (z2 + z), 32, 1)

    part_ref[0] = same(lo, lo2)
    part_ref[1] = same(hi, hi2)
    msg_ref[0] = jnp.where(core == 0, far(lo, lo2) + sides_ref[1], near(lo, lo2))
    msg_ref[1] = jnp.where(core == 1, far(hi, hi2) + sides_ref[0], near(hi, hi2))


def columns_kernel(part_ref, other_ref, own_ref, tail_ref, tab_ref, coef_ref, msg_hbm, sides, msems):
    mx = lax.axis_index("gx")
    low_lanes = lanes(S // 2) < 64
    lo = part_ref[0] + other_ref[0]
    hi = part_ref[1] + other_ref[1]
    top = jnp.where(low_lanes, lo, pltpu.roll(hi, 64, 1))
    bottom = jnp.where(low_lanes, pltpu.roll(lo, 64, 1), hi)
    coef = jnp.concatenate([top, bottom], axis=0)
    coef = coef + tab_ref[TURN] * pltpu.roll(own_ref[...] + tab_ref[HOP_Y] * coef, 96, 1)
    coef_ref[...] = coef
    lane = lanes(S // 2)
    copies = []
    for h in range(2):
        part = pl.ds(h * (S // 2), S // 2)
        at_front, at_back = coef_ref[part, :] * tab_ref[DOWN, part, :], coef_ref[part, :] * tab_ref[UP, part, :]
        front, back = tail_ref[0, part, :], tail_ref[1, part, :]
        for k, table in enumerate(GROUPS):
            inside = (lane >= 32 * k) & (lane < 32 * (k + 1))
            weight = tab_ref[table, part, :]
            front = front + lane_sum(jnp.where(inside, at_front, 0.0)) * weight
            back = back + lane_sum(jnp.where(inside, at_back, 0.0)) * weight
        sides[1, part, :] = front
        sides[0, part, :] = back
        for k in range(8):
            side = (k > mx).astype(jnp.int32)
            target = msg_hbm.at[column_slot(k), part, :]
            copy = pltpu.make_async_copy(sides.at[side, part, :], target, msems.at[h, k])
            copy.start()
            copies.append(copy)
    for copy in copies:
        copy.wait()


def second_kernel(
    b_hbm, adj_ref, cap_ref, cols_ref, tab_ref, mid_hbm, p_hbm, coef_ref, out_hbm,
    out_ref, mid_ref, v_ref, roll_ref, f_ref, b_sems, m_sems, p_sems, o_sems,
):
    def fetch(x):
        column_in(b_hbm, out_ref, b_sems, x).start()
        plane_in(mid_hbm, mid_ref, m_sems, x).start()
        plane_in(p_hbm, v_ref, p_sems, x).start()

    each(0, NXL, fetch)
    cols = cols_ref[...]
    web = food_web(adj_ref, cols)
    rate, d = wide(col(cols, RATE)), wide(col(cols, DEC))
    c = wide(time_step * col(cols, RATE) * col(cols, NORM2))
    ef, eb, alpha, beta = (d * tab_ref[k] for k in (WB, WF, BH, FH))
    e = wide(0.5 * time_step * col(cols, RATE) * col(cols, NORM2))
    roll_ref[...] = coef_ref[...]
    f_ref[...] = jnp.zeros_like(f_ref)

    def response(i, _):
        for j in range(BR):
            x = i * BR + j
            column_in(b_hbm, out_ref, b_sems, x).wait()
            plane_in(mid_hbm, mid_ref, m_sems, x).wait()
            plane_in(p_hbm, v_ref, p_sems, x).wait()
        coef = roll_ref[...]
        roll_ref[...] = pltpu.roll(coef, NYL - BR, 1)
        for j in range(BR):
            x = i * BR + j
            cfu, cfm, cbu, cbm = (coef[:, 32 * k + j : 32 * k + j + 1] for k in range(4))
            mid = mid_ref[x] + c * (cfu * ef + cbu * eb)
            v = v_ref[x] + cfu * alpha + cbu * beta + cfm * ef + cbm * eb
            v_ref[x] = v
            f = v + d * f_ref[...]
            f_ref[...] = f
            rcap = 1.0 / cap_ref[pl.ds(x, 1), :]
            r = respond(mid, rcap, *web)
            out_ref[x] = 0.5 * (out_ref[x] + mid) + 0.5 * time_step * (r - rate * mid) + e * f
        return 0

    lax.fori_loop(0, NXL // BR, response, 0)

    def chunk(i, _):
        part = pl.ds(pl.multiple_of(i * CH, CH), CH)
        d = wide(cols_ref[part, DEC : DEC + 1])
        e = wide(0.5 * time_step * cols_ref[part, RATE : RATE + 1] * cols_ref[part, NORM2 : NORM2 + 1])

        def bwd(k, g):
            for j in range(BX):
                x = NXL - 1 - (k * BX + j)
                g = d * g
                out_ref[x, part, :] = out_ref[x, part, :] + e * g
                g = g + v_ref[x, part, :]
            return g

        lax.fori_loop(0, NXL // BX, bwd, jnp.zeros((CH, NYL), F32))
        chunk_out(out_ref, out_hbm, o_sems, i).start()
        return 0

    lax.fori_loop(0, S // CH, chunk, 0)
    each(0, S // CH, lambda i: chunk_out(out_ref, out_hbm, o_sems, i).wait())


def final_kernel(o_hbm, rx_ref, cols_ref, tab_ref, out_hbm, cf_ref, cb_ref, buf, in_sems, sems):
    loads = [plane_in(o_hbm, buf, in_sems, x) for x in range(NXL)]
    for copy in loads:
        copy.start()
    cols = cols_ref[...]
    lam = col(cols, LAM)
    e = 0.5 * time_step * col(cols, RATE) * col(cols, NORM2)
    cf, cb = read_carries(rx_ref, tab_ref[HOP_X], lax.axis_index("gx"), 8, column_slot)
    cf_ref[...] = cf * (e * col(cols, DEC))
    cb_ref[...] = cb * (e * jnp.exp(-32.0 * lam))
    copies = [pltpu.make_async_copy(buf.at[x], out_hbm.at[:, x, :], sems.at[x]) for x in range(NXL)]
    for x0 in range(0, NXL, BX):
        for x in range(x0, x0 + BX):
            loads[x].wait()
        for s0 in range(0, S, CH):
            part = pl.ds(s0, CH)
            d = wide(cols_ref[part, DEC : DEC + 1])
            inv_d = wide(jnp.exp(cols_ref[part, LAM : LAM + 1]))
            f, g = cf_ref[part, :], cb_ref[part, :]
            for x in range(x0, x0 + BX):
                buf[x, part, :] = buf[x, part, :] + f + g
                f = f * d
                g = g * inv_d
            cf_ref[part, :] = f
            cb_ref[part, :] = g
        for x in range(x0, x0 + BX):
            copies[x].start()
    for copy in copies:
        copy.wait()


VM = pl.BlockSpec(memory_space=pltpu.VMEM)
HBM = pl.BlockSpec(memory_space=pltpu.HBM)
FIELD = (NXL, S, NYL)
PLANE = (S, NYL)


def in_vmem(x):
    return pltpu.with_memory_space_constraint(x, pltpu.VMEM)


def in_hbm(x):
    return pltpu.with_memory_space_constraint(x, pltpu.HBM)


def call(kernel, operands, outs, scratch, microseconds):
    cost = pl.CostEstimate(flops=int(microseconds * 1e9), bytes_accessed=int(microseconds * 2e6), transcendentals=0)
    return pl.pallas_call(
        kernel,
        out_shape=[shape for shape, _ in outs],
        in_specs=[spec for _, spec in operands],
        out_specs=[spec for _, spec in outs],
        scratch_shapes=scratch,
        cost_estimate=cost,
        compiler_params=pltpu.CompilerParams(vmem_limit_bytes=VMEM_LIMIT),
    )(*[in_hbm(x) if spec is HBM else x for x, spec in operands])


def shards(biomass, capacity, adjacency, trophic_level, attack, disp_rate, disp_len):
    field = pltpu.VMEM(FIELD, F32)
    plane = pltpu.VMEM(PLANE, F32)
    columns = pltpu.SemaphoreType.DMA((NXL,))
    chunks = pltpu.SemaphoreType.DMA((S // CH,))
    x_sides = [pltpu.VMEM((2,) + PLANE, F32), pltpu.SemaphoreType.DMA((8,))]
    same_row = [[(k + TURN_BY * (row % 2)) % 8 * 16 + row for k in range(8)] for row in range(16)]
    same_core = [[core + 2 * chip for chip in range(8)] for core in range(2)]
    other_core = [(k, k ^ 1) for k in range(16)]
    field_out = (pltpu.HBM(FIELD, F32), HBM)
    plane_out = (plane, VM)
    x_out = (pltpu.HBM((8,) + PLANE, F32), HBM)
    y_out = (pltpu.HBM((8, S // 2, NYL), F32), HBM)
    halves_out = (pltpu.VMEM((2, S // 2, NYL), F32), VM)
    to_core = (jax.ShapeDtypeStruct((2, S // 2, NYL), F32), VM)
    pair_out = (pltpu.VMEM((2,) + PLANE, F32), VM)
    tables_out = (pltpu.VMEM((10,) + PLANE, F32), VM)
    result = (pltpu.HBM((S, NXL, NYL), F32), HBM)

    vectors = [(v.reshape(1, S), HBM) for v in (trophic_level, attack, disp_rate, disp_len)]
    b = (biomass, HBM)
    adj, cap = (adjacency, VM), (capacity, VM)
    cols, msg = call(
        tails_kernel,
        [b] + vectors,
        [plane_out, x_out],
        [field, pltpu.VMEM((1, S), jnp.int32), pltpu.VMEM((8, S), F32), x_sides[0], columns, pltpu.SemaphoreType.DMA((4,)), x_sides[1]],
        3,
    )
    cols = (in_vmem(cols), VM)
    rx = in_vmem(lax.all_to_all(msg, ("gx", "gy"), 0, 0, axis_index_groups=same_row))
    q, fun, tab = call(
        first_kernel,
        [b, adj, cap, cols],
        [field_out, plane_out, tables_out],
        [field, field, field, plane, columns, columns],
        12,
    )
    tab = (in_vmem(tab), VM)
    car, own, sides, msg = call(
        rows_kernel,
        [(rx, VM), (in_vmem(fun), VM), tab],
        [pair_out, plane_out, halves_out, y_out],
        [pltpu.SemaphoreType.DMA((8,))],
        1,
    )
    ry = in_vmem(lax.all_to_all(msg, "gy", 0, 0, axis_index_groups=same_core))
    mid, p, tail = call(
        local_kernel,
        [(q, HBM), (in_vmem(car), VM), cols],
        [field_out, field_out, pair_out],
        [field, field, plane, plane, columns, columns, columns],
        12,
    )
    part, msg = call(chips_kernel, [(ry, VM), (in_vmem(sides), VM), tab, (in_vmem(tail), VM)], [halves_out, to_core], [], 1)
    other = lax.ppermute(msg, "gy", other_core)
    coef, msg = call(
        columns_kernel, [(in_vmem(part), VM), (other, VM), (in_vmem(own), VM), (in_vmem(tail), VM), tab], [plane_out, x_out], [x_sides[0], pltpu.SemaphoreType.DMA((2, 8))], 1
    )
    rx = in_vmem(lax.all_to_all(msg, ("gx", "gy"), 0, 0, axis_index_groups=same_row))
    (part,) = call(
        second_kernel,
        [b, adj, cap, cols, tab, (mid, HBM), (p, HBM), (in_vmem(coef), VM)],
        [field_out],
        [field, field, field, plane, plane, columns, columns, columns, chunks],
        12,
    )
    (out,) = call(
        final_kernel, [(part, HBM), (rx, VM), cols, tab], [result], [plane, plane, field, columns, columns], 3
    )
    return out


def solution(mesh):
    return jax.shard_map(
        shards,
        mesh=mesh,
        in_specs=(P(None, "gx", "gy"), P("gx", "gy"), P(), P(), P(), P(), P()),
        out_specs=P(None, "gx", "gy"),
        check_vma=False,
    )
```
